256 devices in a mesh: role: 4 (over x_lo, core), fsdp: 64 (over y, x_hi, z).
Axes of the slice: x: 4 (x_hi: 2, x_lo: 2; x = x_hi * 2 + x_lo), y: 4, z: 8, core: 2. Of those that a mesh axis runs over, the one named last changes fastest.
Arguments:
- source_noise: bfloat16 [24576, 64], P('fsdp'), may hold values from -6 to 6
- score_noise: bfloat16 [24576, 64], P('fsdp'), may hold values from -6 to 6
- noise_level: float32 [24576], P('fsdp'), may hold values from 0.05 to 0.95
- embed_weight: bfloat16 [4, 64, 3072], P('role'), may hold values from -0.75 to 0.75
- time_vector: float32 [4, 3072], P('role'), may hold values from -6 to 6
- norm_gain: float32 [4, 3072], P('role'), may hold values from 0.5 to 1.5
- block_weight: bfloat16 [4, 3072, 1536], P('role', 'fsdp'), may hold values from -0.109375 to 0.109375
- readout_weight: bfloat16 [4, 1536, 64], P('role'), may hold values from -0.15625 to 0.15625
Outputs:
- grads: float32 [4, 3072, 1536], P('role', 'fsdp')
- generated: bfloat16 [24576, 64], P('fsdp')
The draws below stay inside these ranges and needn't reach their ends.
All inputs are finite; a program needn't handle non-finite values. Where the reference program divides by a largest or mean magnitude, that divisor is 1e-20 or more.
Results may differ from the reference program's by a relative error of at most 0.0065.
Values may be sent and summed in bfloat16 or wider, within the bound.
A program may use at most 128 MiB of HBM per device.

```python
import math
import jax
import jax.numpy as jnp
from jax import lax

D = 3072
C = 64
F = 1536
TOKENS = 24576
GROUPS = 4


def block_levels(rng, shape, split, smallest, largest):
    factor_of, own = 1.0, jax.random.fold_in(rng, 6)
    for axis_at, parts in split:
        heights = jnp.exp(jax.random.uniform(jax.random.fold_in(own, axis_at), (parts,), jnp.float32, smallest / len(split), largest / len(split)))
        factor_of = factor_of * jnp.repeat(heights, shape[axis_at] // parts).reshape([-1 if axis == axis_at else 1 for axis in range(len(shape))])
    return factor_of


def normal_values(stream_key, extent, scale, bound, split=(), held_as=jnp.bfloat16):
    gain = block_levels(stream_key, extent, split, -0.22, 0.18) if split else 1.0
    array = jax.random.normal(stream_key, extent, jnp.float32) * scale * gain
    return jnp.minimum(jnp.maximum(array, -bound), bound).astype(held_as)


def setup_inputs(seed: int = 0) -> dict:
    arg_keys = jax.random.split(jax.random.key(seed), 9)
    return {
        "source_noise": normal_values(arg_keys[0], (TOKENS, C), 1.0, 6.0, ((0, 64),)),
        "score_noise": normal_values(arg_keys[1], (TOKENS, C), 1.0, 6.0, ((0, 64),)),
        "noise_level": jnp.clip(0.05 + 0.9 * jax.random.uniform(arg_keys[2], (TOKENS,), jnp.float32) ** block_levels(arg_keys[2], (TOKENS,), ((0, 64),), -0.2, 0.2), 0.05, 0.95),
        "embed_weight": normal_values(arg_keys[3], (GROUPS, C, D), C ** -0.5, 0.75, ((0, 4),)),
        "time_vector": normal_values(arg_keys[4], (GROUPS, D), 1.0, 6.0, ((0, 4),), jnp.float32),
        "norm_gain": jnp.clip(1.0 + 0.1 * jax.random.normal(arg_keys[5], (GROUPS, D), jnp.float32), 0.5, 1.5),
        "block_weight": normal_values(arg_keys[6], (GROUPS, D, F), D ** -0.5, 0.109375, ((0, 4), (1, 64))),
        "readout_weight": normal_values(arg_keys[7], (GROUPS, F, C), F ** -0.5, 0.15625, ((0, 4),)),
    }


adv_weight = 3.0

def norm_rows(preact, gain_row):
    return preact * lax.rsqrt(lax.optimization_barrier(jnp.mean(preact * preact, axis=-1, keepdims=True)) + 1e-06) * gain_row

def score_net(latent, level, embed_w, time_w, gain_row, block_w, readout_w):
    preact = jnp.dot(latent, embed_w, preferred_element_type=jnp.float32) + level[:, None] * time_w[None, :]
    normed = norm_rows(preact, gain_row).astype(jnp.bfloat16)
    hidden = jnp.dot(normed, block_w, preferred_element_type=jnp.float32)
    activated = jax.nn.gelu(hidden, approximate=True).astype(jnp.bfloat16)
    output = jnp.dot(activated, readout_w, preferred_element_type=jnp.float32).astype(jnp.bfloat16)
    return (preact, normed, hidden, output)

def hidden_grad(hidden, cotangent, readout_w):
    back = jnp.dot(cotangent, readout_w.astype(jnp.float32).T, precision=lax.Precision.HIGHEST)
    unused, gelu_back = jax.vjp(lambda value: jax.nn.gelu(value, approximate=True), hidden)
    return gelu_back(back)[0].astype(jnp.bfloat16)

def input_grad(hcot, preact, gain_row, block_w, embed_w):
    normed_back = jnp.dot(hcot, block_w.T, preferred_element_type=jnp.float32)
    unused, norm_back = jax.vjp(lambda value: norm_rows(value, gain_row), preact)
    pre_back = norm_back(normed_back)[0]
    return jnp.dot(pre_back, embed_w.astype(jnp.float32).T, precision=lax.Precision.HIGHEST)

def reference(source_noise, score_noise, noise_level, embed_weight, time_vector, norm_gain, block_weight, readout_weight):

    def params(index):
        return (embed_weight[index], time_vector[index], norm_gain[index], block_weight[index], readout_weight[index])
    ones = jnp.ones_like(noise_level)
    pre_gen, normed_gen, hidden_gen, generated = score_net(source_noise, ones, *params(0))
    level = noise_level[:, None]
    noised = ((1.0 - level) * generated.astype(jnp.float32) + level * score_noise.astype(jnp.float32)).astype(jnp.bfloat16)
    unused_a, unused_b, unused_c, real = score_net(noised, noise_level, *params(1))
    unused_d, normed_fake, hidden_fake, fake = score_net(noised, noise_level, *params(2))
    pre_critic, normed_critic, hidden_critic, critic = score_net(noised, noise_level, *params(3))
    gen32 = generated.astype(jnp.float32)
    real32 = real.astype(jnp.float32)
    fake32 = fake.astype(jnp.float32)
    spread = lax.optimization_barrier(jnp.mean(jnp.abs(gen32 - real32), axis=-1, keepdims=True)) + 1e-05
    dmd = ((fake32 - real32) / spread).astype(jnp.bfloat16)
    logit = lax.optimization_barrier(jnp.sum(critic.astype(jnp.float32), axis=-1, keepdims=True))
    adv_cot = jnp.broadcast_to(-jax.nn.sigmoid(-logit), critic.shape)
    adv_hcot = hidden_grad(hidden_critic, adv_cot, readout_weight[3])
    latent_back = input_grad(adv_hcot, pre_critic, norm_gain[3], block_weight[3], embed_weight[3])
    adversarial = (adv_weight * (1.0 - level) * latent_back).astype(jnp.bfloat16)
    push = dmd.astype(jnp.float32) + adversarial.astype(jnp.float32)
    factor = 1.0 / math.sqrt(TOKENS)

    def weight_grad(normed, hidden, cotangent, readout_w):
        hcot = hidden_grad(hidden, cotangent, readout_w)
        return jnp.dot(normed.T, hcot, preferred_element_type=jnp.float32) * factor
    grad_gen = weight_grad(normed_gen, hidden_gen, push, readout_weight[0])
    grad_fake = weight_grad(normed_fake, hidden_fake, fake32 - gen32, readout_weight[2])
    critic_cot = jnp.broadcast_to(jax.nn.sigmoid(logit), critic.shape)
    grad_critic = weight_grad(normed_critic, hidden_critic, critic_cot, readout_weight[3])
    grads = jnp.stack([grad_gen, jnp.zeros_like(grad_gen), grad_fake, grad_critic])
    return (grads, generated)
```

```python
import math

import jax
import jax.numpy as jnp
from jax import lax
from jax.sharding import PartitionSpec as P

adv_weight = 3.0
HIGH = lax.Precision.HIGHEST


def forward(latent, level, lifted, folded, readout_w):
    rows = jnp.concatenate([latent.astype(jnp.float32), level[:, None]], axis=1)
    preact = jnp.dot(rows, lifted, precision=HIGH)
    inverse = lax.rsqrt(jnp.mean(preact * preact, axis=-1, keepdims=True) + 1e-06)
    hidden = inverse * jnp.dot(rows, folded, precision=HIGH)
    activated = jax.nn.gelu(hidden, approximate=True).astype(jnp.bfloat16)
    output = jnp.dot(activated, readout_w, preferred_element_type=jnp.float32).astype(jnp.bfloat16)
    return rows, preact, inverse, hidden, output


def hidden_grad(hidden, cotangent, readout_w):
    back = jnp.dot(cotangent, readout_w.astype(jnp.float32).T, precision=HIGH)
    unused, gelu_back = jax.vjp(lambda value: jax.nn.gelu(value, approximate=True), hidden)
    return gelu_back(back)[0]


def shards(
    source_noise,
    score_noise,
    noise_level,
    embed_weight,
    time_vector,
    norm_gain,
    block_weight,
    readout_weight,
):
    role = lax.axis_index("role")
    place = lax.axis_index("fsdp")
    block_w = block_weight[0]
    depth = block_w.shape[0]
    readout_w = readout_weight[0]
    lifted = jnp.concatenate([embed_weight[0].astype(jnp.float32), time_vector], axis=0)
    own = lax.dynamic_slice_in_dim(lifted * norm_gain, place * depth, depth, axis=1)
    folded = lax.psum(jnp.dot(own, block_w.astype(jnp.float32), precision=HIGH), "fsdp")
    ones = jnp.ones_like(noise_level)
    rows0, pre0, inverse0, hidden0, first = forward(source_noise, ones, lifted, folded, readout_w)
    generated = lax.all_gather(first[None], "role", axis=0, tiled=True)[0]
    gen32 = generated.astype(jnp.float32)
    level = noise_level[:, None]
    noised = ((1.0 - level) * gen32 + level * score_noise.astype(jnp.float32)).astype(jnp.bfloat16)
    rows1, pre1, inverse1, hidden1, scores = forward(
        noised, noise_level, lifted, folded, readout_w
    )
    score32 = scores.astype(jnp.float32)
    logit = jnp.sum(score32, axis=-1, keepdims=True)
    adv_cot = jnp.broadcast_to(-jax.nn.sigmoid(-logit), scores.shape)
    adv_hcot = hidden_grad(hidden1, adv_cot, readout_w).astype(jnp.bfloat16).astype(jnp.float32)
    through = jnp.dot(adv_hcot, folded.T, precision=HIGH)
    pulled = jnp.sum(through * rows1, axis=-1, keepdims=True)
    lift_back = jnp.dot(pre1, lifted[:-1].T, precision=HIGH)
    latent_back = inverse1 * through[:, :-1] - (
        inverse1 * inverse1 * inverse1 / lifted.shape[1] * pulled * lift_back
    )
    adversarial = (adv_weight * (1.0 - level) * latent_back).astype(jnp.bfloat16)
    piece = jnp.where(role == 3, adversarial, scores)
    collected = lax.all_gather(piece[None], "role", axis=0, tiled=True)
    real32 = collected[1].astype(jnp.float32)
    fake32 = collected[2].astype(jnp.float32)
    spread = jnp.mean(jnp.abs(gen32 - real32), axis=-1, keepdims=True) + 1e-05
    dmd = ((fake32 - real32) / spread).astype(jnp.bfloat16)
    push = dmd.astype(jnp.float32) + collected[3].astype(jnp.float32)
    critic_cot = jnp.broadcast_to(jax.nn.sigmoid(logit), scores.shape)
    cotangent = jnp.where(
        role == 0,
        push,
        jnp.where(role == 2, score32 - gen32, jnp.where(role == 3, critic_cot, 0.0)),
    )
    rows = jnp.where(role == 0, rows0, rows1)
    inverse = jnp.where(role == 0, inverse0, inverse1)
    hidden = jnp.where(role == 0, hidden0, hidden1)
    hcot = (inverse * hidden_grad(hidden, cotangent, readout_w)).astype(jnp.bfloat16)
    summed = lax.psum(
        lax.dot_general(
            rows, hcot.astype(jnp.float32), (((0,), (0,)), ((), ())), precision=HIGH
        ),
        "fsdp",
    )
    factor = 1.0 / math.sqrt(source_noise.shape[0] * lax.axis_size("fsdp"))
    grad = lax.dot_general(own * factor, summed, (((0,), (0,)), ((), ())), precision=HIGH)
    return (grad[None], generated)


def solution(mesh):
    in_specs = (
        P("fsdp", None),
        P("fsdp", None),
        P("fsdp"),
        P("role", None, None),
        P("role", None),
        P("role", None),
        P("role", "fsdp", None),
        P("role", None, None),
    )
    out_specs = (P("role", "fsdp", None), P("fsdp", None))
    return jax.shard_map(shards, mesh=mesh, in_specs=in_specs, out_specs=out_specs, check_vma=False)
```

```python
import functools
import math

import jax
import jax.numpy as jnp
from jax import lax
from jax.experimental import pallas as pl
from jax.experimental.pallas import tpu as pltpu
from jax.sharding import PartitionSpec as P

MESH = pl.DeviceIdType.MESH
f32, bf16 = jnp.float32, jnp.bfloat16
adv_weight = 3.0
ROWS = 384
C = 64
D = 3072
F = 1536
DEPTH = 48
CHUNK = 256
CHUNKS = F // CHUNK
SIDE = 8
HALF = F // 2
ROOT = math.sqrt(2.0 / math.pi)
CUBE = 0.044715 * ROOT


def dot(a, b):
    return jnp.dot(a, b, preferred_element_type=f32)


def dot_nt(a, b):
    return lax.dot_general(a, b, (((1,), (1,)), ((), ())), preferred_element_type=f32)


def split(value):
    high = value.astype(bf16)
    return high, (value - high.astype(f32)).astype(bf16)


def lanes(shape):
    return lax.broadcasted_iota(jnp.int32, shape, len(shape) - 1)


def pack(value):
    top, bottom = value[: ROWS // 2], value[ROWS // 2 :]
    return jnp.where(lanes(top.shape) < C, top, bottom)


def unpack(value):
    turned = pltpu.roll(value, C, 1)
    left = lanes(value.shape) < C
    return jnp.concatenate([jnp.where(left, value, turned), jnp.where(left, turned, value)], axis=0)


def gelu_parts(hidden):
    square = hidden * hidden
    half = 0.5 + 0.5 * jnp.tanh(hidden * (ROOT + CUBE * square))
    return square, half, hidden * half


def gelu_slope(square, half, value):
    return half + value * (1.0 - half) * (2.0 * ROOT + 6.0 * CUBE * square)


def kernel(
    sn, sc, lv, emb, tim, gain, blk, rdo,
    grads, gen_out,
    x_ref, vt, vrow, s_a, d_a, s_b, d_b, m_buf, m_aug,
    t_a, e_a, t_b, e_b, h_buf,
    r2, gram, level, z_f32, z_aug, z_t, rs, y_ref, hid, slope, acc, back_acc, lt, cot,
    gen_pk, gen_in, out_pk, col_in,
    send_m, recv_m, send_h, recv_h, send_g, recv_g, send_c, recv_c,
):
    role = lax.axis_index("role")
    place = lax.axis_index("fsdp")
    p, z = place // SIDE, place % SIDE

    def yx_peer(k):
        return (role, lax.rem(p + k, SIDE) * SIDE + z)

    def z_peer(k):
        return (role, p * SIDE + lax.rem(z + k, SIDE))

    def role_peer(k):
        return (lax.rem(role + k, 4), place)

    barrier = pltpu.get_barrier_semaphore()
    for k in range(1, SIDE):
        pl.semaphore_signal(barrier, inc=1, device_id=yx_peer(k), device_id_type=MESH)
        pl.semaphore_signal(barrier, inc=1, device_id=z_peer(k), device_id_type=MESH)
    for k in range(1, 4):
        pl.semaphore_signal(barrier, inc=1, device_id=role_peer(k), device_id_type=MESH)

    def remote(src, dst, send, recv, device):
        return pltpu.make_async_remote_copy(
            src_ref=src, dst_ref=dst, send_sem=send, recv_sem=recv, device_id=device,
            device_id_type=MESH,
        )

    begin = place * DEPTH
    window = jnp.minimum(begin // 128, D // 128 - 2) * 128
    window = pl.multiple_of(window, 128)
    wide = pl.ds(window, 256)
    gain_w = gain[:, wide]
    lifted = jnp.concatenate(
        [
            emb[0, :, wide].astype(f32) * gain_w,
            jnp.where(
                lax.broadcasted_iota(jnp.int32, (16, 256), 0) == 0, tim[:, wide] * gain_w, 0.0
            ),
        ],
        axis=0,
    )
    lifted = pltpu.roll(lifted, lax.rem(256 + window - begin, 256), 1)[:, :128]
    high, low = split(lifted[:, :DEPTH])
    block = blk[0]
    x_ref[...] = dot(high, block) + dot(low, block)

    def stage_a_fill(send, wide_type):
        vt[...] = jnp.zeros_like(vt)
        for i in range(F // 128):
            vt[i : i + 1, :] = x_ref[C : C + 1, i * 128 : i * 128 + 128]
        tile = vt[...]
        for piece in range(SIDE):
            top, left = piece // 2 * 16, piece % 2 * HALF
            part = x_ref[top : top + 16, left : left + HALF]
            if wide_type:
                send[piece, :, :HALF] = part
                send[piece, :, HALF:] = tile
            else:
                send[piece, :, :HALF] = part.astype(bf16)
                v_high, v_low = split(tile)
                send[piece, :, HALF : HALF + 128] = v_high
                send[piece, :, HALF + 128 :] = v_low

    def stage_a(send, dest, ss, rr):
        return [
            remote(send.at[lax.rem(p + k, SIDE)], dest.at[k], ss.at[0, k], rr.at[0, k], yx_peer(k))
            for k in range(1, SIDE)
        ]

    def stage_b(send, dest, ss, rr):
        return [
            remote(send, dest.at[k], ss.at[1, k], rr.at[1, k], z_peer(k)) for k in range(1, SIDE)
        ]

    own_top = pl.multiple_of(p // 2 * 16, 16)
    own_left = pl.multiple_of(lax.rem(p, 2) * HALF, 128)

    def stage_c(buf, ss, rr):
        own = buf.at[pl.ds(own_top, 16), pl.ds(own_left, HALF)]
        return [remote(own, own, ss.at[2, k], rr.at[2, k], yx_peer(k)) for k in range(1, SIDE)]

    def start(copies):
        for copy in copies:
            copy.start()

    def arrive(copies):
        for copy in copies:
            copy.wait_recv()

    def finish(copies):
        for copy in copies:
            copy.wait_send()

    def total(first, dest):
        value = first.astype(f32)
        for k in range(1, SIDE):
            value = value + dest[k].astype(f32)
        return value

    def put_row(tile):
        vt[...] = tile
        for i in range(F // 128):
            vrow[0:1, i * 128 : i * 128 + 128] = vt[i : i + 1, :]

    stage_a_fill(s_a, True)
    pl.semaphore_wait(barrier, 2 * (SIDE - 1) + 3)
    m_a = stage_a(s_a, d_a, send_m, recv_m)
    start(m_a)

    lt[...] = jnp.concatenate([lifted, jnp.zeros((48, 128), f32)], axis=0).T[:DEPTH]
    for i in range(ROWS // 128):
        level[i * 128 : i * 128 + 128, :] = jnp.broadcast_to(lv[i : i + 1, :], (128, 128)).T
    readout = rdo[0].astype(f32)
    r2[...] = jnp.concatenate([readout, readout], axis=1).astype(bf16)
    time = tim[...]
    t_1 = time.astype(bf16).astype(f32)
    t_2 = (time - t_1).astype(bf16).astype(f32)
    t_3 = time - t_1 - t_2
    rows = lax.broadcasted_iota(jnp.int32, (16, D), 0)
    parts = jnp.where(rows == 0, t_1, jnp.where(rows == 1, t_2, jnp.where(rows == 2, t_3, 0.0)))
    square_e = dot_nt(emb[0], emb[0])
    cross = jnp.sum(dot_nt(parts.astype(bf16), emb[0]), axis=0, keepdims=True)
    square_e = jnp.concatenate([square_e, square_e], axis=1)
    cross = jnp.concatenate([cross, cross], axis=1)
    square_t = jnp.sum(time * time, axis=1, keepdims=True)
    g_1, rest = split(square_e)
    rest = square_e - g_1.astype(f32)
    g_2, g_3 = split(rest)
    gram[0:64, :] = g_1
    gram[64:128, :] = g_2
    gram[128:192, :] = g_3
    gram[192:256, :] = jnp.zeros((64, 128), bf16)

    def rows_in(latent, lev):
        lane = lanes((ROWS, 128))
        lev_high = lev.astype(bf16).astype(f32)
        lev_low = lev - lev_high
        z_f32[...] = latent
        latent16 = latent.astype(bf16)
        z_aug[:, :128] = latent16
        z_aug[:, 128:] = jnp.where(
            lane < 2, lev_high, jnp.where(lane == 2, lev_low, 0.0)
        ).astype(bf16)
        y = (
            dot(latent16, gram[0:128, :]) + dot(latent16, gram[128:256, :]) + lev * cross
        )
        y_ref[...] = y
        mean = (
            0.5 * jnp.sum(latent * (y + lev * cross), axis=1, keepdims=True)
            + lev[:, :1] * lev[:, :1] * square_t
        ) * (1.0 / D)
        rs[...] = jnp.broadcast_to(lax.rsqrt(jnp.maximum(mean, 0.0) + 1e-06), (ROWS, CHUNK))

    def rows_turned():
        lane = lanes((ROWS, 128))
        lev = jnp.where(role == 0, 1.0, level[...])
        lev_high = lev.astype(bf16).astype(f32)
        lev_low = lev - lev_high
        turned = jnp.where(
            lane < C, z_f32[...], jnp.where(lane == C, lev_high, jnp.where(lane == C + 1, lev_low, 0.0))
        ).T
        z_t[...] = turned[:80].astype(bf16)

    arrive(m_a)
    summed = total(s_a[p], d_a)
    s_b[...] = summed
    m_b = stage_b(s_b, d_b, send_m, recv_m)
    start(m_b)
    m_aug[128 + 16 :, :] = jnp.zeros((128 - 16, F), bf16)

    @pl.when(role == 0)
    def _():
        noise = sn[...].astype(f32)
        rows_in(jnp.concatenate([noise, noise], axis=1), jnp.ones((ROWS, 128), f32))

    arrive(m_b)
    summed = total(summed, d_b)
    m_buf[pl.ds(own_top, 16), pl.ds(own_left, HALF)] = summed[:, :HALF]
    m_c = stage_c(m_buf, send_m, recv_m)
    start(m_c)
    put_row(summed[:, HALF:])
    v_full = vrow[0:1, :]
    v_high = v_full.astype(bf16).astype(f32)
    rows = lax.broadcasted_iota(jnp.int32, (16, F), 0)
    m_aug[128:144, :] = jnp.where(
        (rows == 0) | (rows == 2), v_high, jnp.where(rows == 1, v_full - v_high, 0.0)
    ).astype(bf16)
    arrive(m_c)
    high, low = split(m_buf[...])
    m_aug[0:64, :] = high
    m_aug[64:128, :] = low
    finish(m_a)
    finish(m_b)
    finish(m_c)

    def columns(c):
        return pl.ds(pl.multiple_of(c * CHUNK, CHUNK), CHUNK)

    def forward(critic):
        acc[...] = jnp.zeros_like(acc)
        if critic:
            back_acc[...] = jnp.zeros_like(back_acc)

        def body(c, carry):
            cs = columns(c)
            hidden = dot(z_aug[...], m_aug[:, cs]) * rs[...]
            square, half, value = gelu_parts(hidden)
            acc[...] += dot(value.astype(bf16), r2[cs, :])
            if critic:
                rise = gelu_slope(square, half, value)
                slope[:, cs] = rise * rs[...]
                weight = dot_nt(jnp.ones((16, C), bf16), rdo[0, cs, :])[0:1, :]
                back_acc[...] += dot_nt((rise * weight).astype(bf16), m_aug[:, cs])
            else:
                hid[:, cs] = hidden
            return carry

        lax.fori_loop(0, CHUNKS, body, 0)
        return acc[...].astype(bf16).astype(f32)

    def slopes():
        def body(c, carry):
            cs = columns(c)
            slope[:, cs] = gelu_slope(*gelu_parts(hid[:, cs])) * rs[...]
            return carry

        lax.fori_loop(0, CHUNKS, body, 0)

    to_gen = (0, place)

    @pl.when(role == 0)
    def _():
        out = forward(False)
        gen_pk[...] = pack(out).astype(bf16)
        copies = [
            remote(gen_pk, gen_in, send_g.at[k], recv_g.at[0], (k, place)) for k in range(1, 4)
        ]
        start(copies)
        gen_out[...] = out[:, :C].astype(bf16)
        slopes()
        rows_turned()
        finish(copies)
        sources = [
            remote(out_pk, col_in.at[k], send_c.at[0], recv_c.at[k], (k, place))
            for k in range(1, 4)
        ]
        arrive(sources)
        real = unpack(col_in[1].astype(f32))
        fake = unpack(col_in[2].astype(f32))
        adversarial = unpack(col_in[3].astype(f32))
        spread = jnp.sum(jnp.abs(out - real), axis=1, keepdims=True) * (0.5 / C) + 1e-05
        dmd = ((fake - real) / spread).astype(bf16).astype(f32)
        cot[...] = dmd + adversarial

    @pl.when(role != 0)
    def _():
        remote(gen_pk, gen_in, send_g.at[0], recv_g.at[0], to_gen).wait_recv()
        gen32 = unpack(gen_in[...].astype(f32))
        gen_out[...] = gen32[:, :C].astype(bf16)
        noise = sc[...].astype(f32)
        lev = level[...]
        noised = (1.0 - lev) * gen32 + lev * jnp.concatenate([noise, noise], axis=1)
        rows_in(noised.astype(bf16).astype(f32), lev)

        def deliver(value):
            out_pk[...] = pack(value).astype(bf16)
            copy = remote(out_pk, col_in.at[role], send_c.at[0], recv_c.at[role], to_gen)
            copy.start()
            return copy

        @pl.when(role == 3)
        def _():
            out = forward(True)
            logit = 0.5 * jnp.sum(out, axis=1, keepdims=True)
            down = -1.0 / (1.0 + jnp.exp(logit))
            through = back_acc[...]
            pulled = jnp.sum(z_aug[...].astype(f32) * through, axis=1, keepdims=True)
            latent = through[:, :128]
            latent = latent + pltpu.roll(latent, C, 1)
            inverse = rs[:, :128]
            back = inverse * latent - inverse * inverse * inverse * (1.0 / D) * pulled * y_ref[...]
            copy = deliver(adv_weight * (1.0 - level[...]) * down * back)
            cot[...] = jnp.broadcast_to(1.0 / (1.0 + jnp.exp(-logit)), (ROWS, 128))
            rows_turned()
            copy.wait_send()

        @pl.when(role != 3)
        def _():
            out = forward(False)
            copy = deliver(out)
            cot[...] = out - gen32

            @pl.when(role == 2)
            def _():
                slopes()
                rows_turned()

            copy.wait_send()

    @pl.when(role == 1)
    def _():
        grads[...] = jnp.zeros_like(grads)

    @pl.when(role != 1)
    def _():
        lane = lanes((ROWS, 128))
        full = cot[...]
        c_high = full.astype(bf16).astype(f32)
        cot2 = jnp.where(lane < C, c_high, full - c_high).astype(bf16)

        def body(c, carry):
            cs = columns(c)
            hcot = (dot_nt(cot2, r2[cs, :]) * slope[:, cs]).astype(bf16)
            x_ref[:, cs] = dot(z_t[...], hcot)
            return carry

        lax.fori_loop(0, CHUNKS, body, 0)
        x_ref[C : C + 1, :] = x_ref[C : C + 1, :] + x_ref[C + 1 : C + 2, :]
        stage_a_fill(t_a, False)
        h_a = stage_a(t_a, e_a, send_h, recv_h)
        start(h_a)
        arrive(h_a)
        summed = total(t_a[p], e_a)
        t_b[:, :HALF] = summed[:, :HALF].astype(bf16)
        v_high, v_low = split(summed[:, HALF : HALF + 128] + summed[:, HALF + 128 :])
        t_b[:, HALF : HALF + 128] = v_high
        t_b[:, HALF + 128 :] = v_low
        h_b = stage_b(t_b, e_b, send_h, recv_h)
        start(h_b)
        arrive(h_b)
        summed = total(summed, e_b)
        h_buf[pl.ds(own_top, 16), pl.ds(own_left, HALF)] = summed[:, :HALF].astype(bf16)
        h_c = stage_c(h_buf, send_h, recv_h)
        start(h_c)
        put_row(summed[:, HALF : HALF + 128] + summed[:, HALF + 128 :])
        left = lt[...] * (1.0 / math.sqrt(ROWS * SIDE * SIDE))
        l_high, l_low = split(left[:, :C])
        base = left[:, C : C + 1] * vrow[0:1, :]
        arrive(h_c)
        full_h = h_buf[...]
        grads[0] = base + dot(l_high, full_h) + dot(l_low, full_h)
        finish(h_a)
        finish(h_b)
        finish(h_c)


def shards(sn, sc, lv, emb, tim, gain, blk, rdo):
    vmem = pl.BlockSpec(memory_space=pltpu.VMEM)
    scratch = [
        ((80, F), f32), ((16, 128), f32), ((8, F), f32),
        ((SIDE, 16, HALF + 128), f32), ((SIDE, 16, HALF + 128), f32),
        ((16, HALF + 128), f32), ((SIDE, 16, HALF + 128), f32),
        ((C, F), f32), ((256, F), bf16),
        ((SIDE, 16, HALF + 256), bf16), ((SIDE, 16, HALF + 256), bf16),
        ((16, HALF + 256), bf16), ((SIDE, 16, HALF + 256), bf16), ((C, F), bf16),
        ((F, 128), bf16), ((256, 128), bf16), ((ROWS, 128), f32), ((ROWS, 128), f32),
        ((ROWS, 256), bf16), ((80, ROWS), bf16), ((ROWS, CHUNK), f32), ((ROWS, 128), f32),
        ((ROWS, F), f32), ((ROWS, F), f32), ((ROWS, 128), f32), ((ROWS, 256), f32),
        ((DEPTH, 128), f32), ((ROWS, 128), f32),
        ((ROWS // 2, 128), bf16), ((ROWS // 2, 128), bf16), ((ROWS // 2, 128), bf16),
        ((4, ROWS // 2, 128), bf16),
    ]
    dma = pltpu.SemaphoreType.DMA
    return pl.pallas_call(
        kernel,
        out_shape=(
            jax.ShapeDtypeStruct((1, DEPTH, F), f32),
            jax.ShapeDtypeStruct((ROWS, C), bf16),
        ),
        in_specs=[vmem] * 8,
        out_specs=(vmem, vmem),
        scratch_shapes=[pltpu.VMEM(shape, kind) for shape, kind in scratch]
        + [dma((3, SIDE)) for _ in range(4)]
        + [dma((4,)) for _ in range(4)],
        compiler_params=pltpu.CompilerParams(
            collective_id=0, has_side_effects=True, vmem_limit_bytes=48 * 2**20
        ),
    )(sn, sc, lv.reshape(ROWS // 128, 128), emb, tim, gain, blk, rdo)


def solution(mesh):
    in_specs = (
        P("fsdp", None),
        P("fsdp", None),
        P("fsdp"),
        P("role", None, None),
        P("role", None),
        P("role", None),
        P("role", "fsdp", None),
        P("role", None, None),
    )
    out_specs = (P("role", "fsdp", None), P("fsdp", None))
    return jax.shard_map(shards, mesh=mesh, in_specs=in_specs, out_specs=out_specs, check_vma=False)
```

```python
import functools
import math

import jax
import jax.numpy as jnp
from jax import lax
from jax.experimental import pallas as pl
from jax.experimental.pallas import tpu as pltpu
from jax.sharding import PartitionSpec as P

MESH = pl.DeviceIdType.MESH
f32, bf16 = jnp.float32, jnp.bfloat16
adv_weight = 3.0
ROWS = 384
C = 64
D = 3072
F = 1536
DEPTH = 48
CHUNK = 256
CHUNKS = F // CHUNK
SIDE = 8
HALF = F // 2
YX_ORDER = (5, 3, 4, 7, 1, 6, 2)
Z_ORDER = (4, 5, 3, 6, 2, 7, 1)
ROOT = math.sqrt(2.0 / math.pi)
CUBE = 0.044715 * ROOT


def dot(a, b):
    return jnp.dot(a, b, preferred_element_type=f32)


def dot_nt(a, b):
    return lax.dot_general(a, b, (((1,), (1,)), ((), ())), preferred_element_type=f32)


def split(value):
    high = value.astype(bf16)
    return high, (value - high.astype(f32)).astype(bf16)


def lanes(shape):
    return lax.broadcasted_iota(jnp.int32, shape, len(shape) - 1)


def pack(value):
    top, bottom = value[: ROWS // 2], value[ROWS // 2 :]
    return jnp.where(lanes(top.shape) < C, top, bottom)


def unpack(value):
    turned = pltpu.roll(value, C, 1)
    left = lanes(value.shape) < C
    return jnp.concatenate([jnp.where(left, value, turned), jnp.where(left, turned, value)], axis=0)


def gelu_parts(hidden):
    square = hidden * hidden
    half = 0.5 + 0.5 * jnp.tanh(hidden * (ROOT + CUBE * square))
    return square, half, hidden * half


def gelu_slope(square, half, value):
    return half + value * (1.0 - half) * (2.0 * ROOT + 6.0 * CUBE * square)


def kernel(
    *refs,
):
    hbm, (grads, gen_out), scratch, (fetch, *sems) = refs[:8], refs[8:10], refs[10:-10], refs[-10:]
    step(hbm, fetch, grads, gen_out, *scratch, *sems)


def step(
    hbm, fetch, grads, gen_out,
    sn, sc, lv, emb, tim, gain, blk, rdo, x_ref, vt, vrow, s_a, d_a, s_b, d_b, m_buf, m_aug,
    t_a, e_a, t_b, e_b, h_buf,
    r2, gram, level, z_f32, z_aug, z_t, rs, y_ref, hid, slope, acc, back_acc, lt, cot,
    noise_in, gen_pk, gen_in, out_pk, col_in,
    send_m, recv_m, send_h, recv_h, send_g, recv_g, send_c, recv_c, turn,
):
    role = lax.axis_index("role")
    place = lax.axis_index("fsdp")
    p, z = place // SIDE, place % SIDE

    def yx_peer(k):
        return (role, lax.rem(p + k, SIDE) * SIDE + z)

    def z_peer(k):
        return (role, p * SIDE + lax.rem(z + k, SIDE))

    def role_peer(k):
        return (lax.rem(role + k, 4), place)

    barrier = pltpu.get_barrier_semaphore()
    for k_yx, k_z in zip(YX_ORDER, Z_ORDER):
        pl.semaphore_signal(barrier, inc=1, device_id=yx_peer(k_yx), device_id_type=MESH)
        pl.semaphore_signal(barrier, inc=1, device_id=z_peer(k_z), device_id_type=MESH)
    for k in range(1, 4):
        pl.semaphore_signal(barrier, inc=1, device_id=role_peer(k), device_id_type=MESH)

    fetches = [
        pltpu.make_async_copy(src, dst, fetch.at[i])
        for i, (src, dst) in enumerate(zip(hbm, (sn, sc, lv, emb, tim, gain, blk, rdo)))
    ]
    for i in (4, 5, 3, 6, 7, 0, 1, 2):
        fetches[i].start()

    def remote(src, dst, send, recv, device):
        return pltpu.make_async_remote_copy(
            src_ref=src, dst_ref=dst, send_sem=send, recv_sem=recv, device_id=device,
            device_id_type=MESH,
        )

    begin = place * DEPTH
    window = jnp.minimum(begin // 128, D // 128 - 2) * 128
    window = pl.multiple_of(window, 128)
    wide = pl.ds(window, 256)
    for i in (4, 5, 3, 6):
        fetches[i].wait()
    gain_w = gain[:, wide]
    lifted = jnp.concatenate(
        [
            emb[0, :, wide].astype(f32) * gain_w,
            jnp.where(
                lax.broadcasted_iota(jnp.int32, (16, 256), 0) == 0, tim[:, wide] * gain_w, 0.0
            ),
        ],
        axis=0,
    )
    lifted = pltpu.roll(lifted, lax.rem(256 + window - begin, 256), 1)[:, :128]
    high, low = split(lifted[:, :DEPTH])
    block = blk[0]
    x_ref[...] = dot(high, block) + dot(low, block)

    def stage_a_fill(send, wide_type):
        vt[...] = jnp.zeros_like(vt)
        for i in range(F // 128):
            vt[i : i + 1, :] = x_ref[C : C + 1, i * 128 : i * 128 + 128]
        tile = vt[...]
        for piece in range(SIDE):
            top, left = piece // 2 * 16, piece % 2 * HALF
            part = x_ref[top : top + 16, left : left + HALF]
            if wide_type:
                send[piece, :, :HALF] = part
                send[piece, :, HALF:] = tile
            else:
                send[piece, :, :HALF] = part.astype(bf16)
                v_high, v_low = split(tile)
                send[piece, :, HALF : HALF + 128] = v_high
                send[piece, :, HALF + 128 :] = v_low

    def stage_a(send, dest, ss, rr):
        return [
            remote(send.at[lax.rem(p + k, SIDE)], dest.at[k], ss.at[0, k], rr.at[0, k], yx_peer(k))
            for k in YX_ORDER
        ]

    def stage_b(send, dest, ss, rr):
        return [
            remote(send, dest.at[k], ss.at[1, k], rr.at[1, k], z_peer(k)) for k in Z_ORDER
        ]

    own_top = pl.multiple_of(p // 2 * 16, 16)
    own_left = pl.multiple_of(lax.rem(p, 2) * HALF, 128)

    def stage_c(buf, ss, rr):
        own = buf.at[pl.ds(own_top, 16), pl.ds(own_left, HALF)]
        return [remote(own, own, ss.at[2, k], rr.at[2, k], yx_peer(k)) for k in YX_ORDER]

    def start(copies):
        for copy in copies:
            copy.start()

    def arrive(copies):
        for copy in copies:
            copy.wait_recv()

    def finish(copies):
        for copy in copies:
            copy.wait_send()

    def total(first, dest):
        value = first.astype(f32)
        for k in range(1, SIDE):
            value = value + dest[k].astype(f32)
        return value

    def put_row(tile):
        vt[...] = tile
        for i in range(F // 128):
            vrow[0:1, i * 128 : i * 128 + 128] = vt[i : i + 1, :]

    stage_a_fill(s_a, True)
    pl.semaphore_wait(barrier, 2 * (SIDE - 1) + 3)
    m_a = stage_a(s_a, d_a, send_m, recv_m)

    @pl.when((role == 1) | (role == 2))
    def _():
        pl.semaphore_wait(turn, 1)

    start(m_a)

    for i in (0, 1, 2, 7):
        fetches[i].wait()

    lt[...] = jnp.concatenate([lifted, jnp.zeros((48, 128), f32)], axis=0).T[:DEPTH]
    for i in range(ROWS // 128):
        level[i * 128 : i * 128 + 128, :] = jnp.broadcast_to(lv[i : i + 1, :], (128, 128)).T
    readout = rdo[0].astype(f32)
    r2[...] = jnp.concatenate([readout, readout], axis=0).T.astype(bf16)
    time = tim[...]
    t_1 = time.astype(bf16).astype(f32)
    t_2 = (time - t_1).astype(bf16).astype(f32)
    t_3 = time - t_1 - t_2
    rows = lax.broadcasted_iota(jnp.int32, (16, D), 0)
    parts = jnp.where(rows == 0, t_1, jnp.where(rows == 1, t_2, jnp.where(rows == 2, t_3, 0.0)))
    square_e = dot_nt(emb[0], emb[0])
    cross = jnp.sum(dot_nt(parts.astype(bf16), emb[0]), axis=0, keepdims=True)
    square_e = jnp.concatenate([square_e, square_e], axis=1)
    cross = jnp.concatenate([cross, cross], axis=1)
    square_t = jnp.sum(time * time, axis=1, keepdims=True)
    g_1, rest = split(square_e)
    rest = square_e - g_1.astype(f32)
    g_2, g_3 = split(rest)
    gram[0:64, :] = g_1
    gram[64:128, :] = g_2
    gram[128:192, :] = g_3
    gram[192:256, :] = jnp.zeros((64, 128), bf16)

    def rows_in(latent, lev):
        lane = lanes((ROWS, 128))
        lev_high = lev.astype(bf16).astype(f32)
        lev_low = lev - lev_high
        z_f32[...] = latent
        latent16 = latent.astype(bf16)
        z_aug[:, :128] = latent16
        z_aug[:, 128:] = jnp.where(
            lane < 2, lev_high, jnp.where(lane == 2, lev_low, 0.0)
        ).astype(bf16)
        y = (
            dot(latent16, gram[0:128, :]) + dot(latent16, gram[128:256, :]) + lev * cross
        )
        y_ref[...] = y
        mean = (
            0.5 * jnp.sum(latent * (y + lev * cross), axis=1, keepdims=True)
            + lev[:, :1] * lev[:, :1] * square_t
        ) * (1.0 / D)
        rs[...] = jnp.broadcast_to(lax.rsqrt(jnp.maximum(mean, 0.0) + 1e-06), (ROWS, CHUNK))

    def rows_turned():
        lane = lanes((ROWS, 128))
        lev = jnp.where(role == 0, 1.0, level[...])
        lev_high = lev.astype(bf16).astype(f32)
        lev_low = lev - lev_high
        turned = jnp.where(
            lane < C, z_f32[...], jnp.where(lane == C, lev_high, jnp.where(lane == C + 1, lev_low, 0.0))
        ).T
        z_t[...] = turned[:80].astype(bf16)

    arrive(m_a)

    @pl.when((role == 0) | (role == 3))
    def _():
        pl.semaphore_signal(
            turn, inc=1, device_id=(jnp.where(role == 0, 1, 2), place), device_id_type=MESH
        )

    summed = total(s_a[p], d_a)
    s_b[...] = summed
    m_b = stage_b(s_b, d_b, send_m, recv_m)
    start(m_b)
    m_aug[128 + 16 :, :] = jnp.zeros((128 - 16, F), bf16)

    @pl.when(role == 0)
    def _():
        noise = sn[...].astype(f32)
        rows_in(jnp.concatenate([noise, noise], axis=0).T, jnp.ones((ROWS, 128), f32))

    @pl.when(role != 0)
    def _():
        noise = sc[...].astype(f32)
        noise_in[...] = level[...] * jnp.concatenate([noise, noise], axis=0).T

    arrive(m_b)
    summed = total(summed, d_b)
    m_buf[pl.ds(own_top, 16), pl.ds(own_left, HALF)] = summed[:, :HALF]
    m_c = stage_c(m_buf, send_m, recv_m)
    start(m_c)
    put_row(summed[:, HALF:])
    v_full = vrow[0:1, :]
    v_high = v_full.astype(bf16).astype(f32)
    rows = lax.broadcasted_iota(jnp.int32, (16, F), 0)
    m_aug[128:144, :] = jnp.where(
        (rows == 0) | (rows == 2), v_high, jnp.where(rows == 1, v_full - v_high, 0.0)
    ).astype(bf16)
    arrive(m_c)
    high, low = split(m_buf[...])
    m_aug[0:64, :] = high
    m_aug[64:128, :] = low
    finish(m_a)
    finish(m_b)
    finish(m_c)

    def columns(c):
        return pl.ds(pl.multiple_of(c * CHUNK, CHUNK), CHUNK)

    def forward(critic):
        acc[...] = jnp.zeros_like(acc)
        if critic:
            back_acc[...] = jnp.zeros_like(back_acc)

        def body(c, carry):
            cs = columns(c)
            hidden = dot(z_aug[...], m_aug[:, cs]) * rs[...]
            square, half, value = gelu_parts(hidden)
            acc[...] += dot(value.astype(bf16), r2[cs, :])
            if critic:
                rise = gelu_slope(square, half, value)
                slope[:, cs] = rise * rs[...]
                weight = dot(jnp.ones((16, C), bf16), rdo[0, :, cs])[0:1, :]
                back_acc[...] += dot_nt((rise * weight).astype(bf16), m_aug[:, cs])
            else:
                hid[:, cs] = hidden
            return carry

        lax.fori_loop(0, CHUNKS, body, 0, unroll=6)
        return acc[...].astype(bf16).astype(f32)

    def slopes():
        def body(c, carry):
            cs = columns(c)
            slope[:, cs] = gelu_slope(*gelu_parts(hid[:, cs])) * rs[...]
            return carry

        lax.fori_loop(0, CHUNKS, body, 0, unroll=6)

    to_gen = (0, place)

    @pl.when(role == 0)
    def _():
        out = forward(False)
        gen_pk[...] = pack(out).astype(bf16)
        copies = [
            remote(gen_pk, gen_in, send_g.at[k], recv_g.at[0], (k, place)) for k in range(1, 4)
        ]
        start(copies)
        gen_out[...] = out.T[:C].astype(bf16)
        slopes()
        rows_turned()
        finish(copies)
        sources = [
            remote(out_pk, col_in.at[k], send_c.at[0], recv_c.at[k], (k, place))
            for k in range(1, 4)
        ]
        arrive(sources)
        real = unpack(col_in[1].astype(f32))
        fake = unpack(col_in[2].astype(f32))
        adversarial = unpack(col_in[3].astype(f32))
        spread = jnp.sum(jnp.abs(out - real), axis=1, keepdims=True) * (0.5 / C) + 1e-05
        dmd = ((fake - real) / spread).astype(bf16).astype(f32)
        cot[...] = dmd + adversarial

    @pl.when(role != 0)
    def _():
        remote(gen_pk, gen_in, send_g.at[0], recv_g.at[0], to_gen).wait_recv()
        gen32 = unpack(gen_in[...].astype(f32))
        lev = level[...]
        noised = (1.0 - lev) * gen32 + noise_in[...]
        rows_in(noised.astype(bf16).astype(f32), lev)

        def deliver(value):
            out_pk[...] = pack(value).astype(bf16)
            copy = remote(out_pk, col_in.at[role], send_c.at[0], recv_c.at[role], to_gen)
            copy.start()
            return copy

        @pl.when(role == 3)
        def _():
            out = forward(True)
            logit = 0.5 * jnp.sum(out, axis=1, keepdims=True)
            down = -1.0 / (1.0 + jnp.exp(logit))
            through = back_acc[...]
            pulled = jnp.sum(z_aug[...].astype(f32) * through, axis=1, keepdims=True)
            latent = through[:, :128]
            latent = latent + pltpu.roll(latent, C, 1)
            inverse = rs[:, :128]
            back = inverse * latent - inverse * inverse * inverse * (1.0 / D) * pulled * y_ref[...]
            copy = deliver(adv_weight * (1.0 - level[...]) * down * back)
            gen_out[...] = gen32.T[:C].astype(bf16)
            cot[...] = jnp.broadcast_to(1.0 / (1.0 + jnp.exp(-logit)), (ROWS, 128))
            rows_turned()
            copy.wait_send()

        @pl.when(role != 3)
        def _():
            out = forward(False)
            copy = deliver(out)
            gen_out[...] = gen32.T[:C].astype(bf16)
            cot[...] = out - gen32

            @pl.when(role == 2)
            def _():
                slopes()
                rows_turned()

            copy.wait_send()

    @pl.when(role == 1)
    def _():
        grads[...] = jnp.zeros_like(grads)

    @pl.when(role != 1)
    def _():
        lane = lanes((ROWS, 128))
        full = cot[...]
        c_high = full.astype(bf16).astype(f32)
        cot2 = jnp.where(lane < C, c_high, full - c_high).astype(bf16)

        def body(c, carry):
            cs = columns(c)
            hcot = (dot_nt(cot2, r2[cs, :]) * slope[:, cs]).astype(bf16)
            x_ref[:, cs] = dot(z_t[...], hcot)
            return carry

        lax.fori_loop(0, CHUNKS, body, 0, unroll=6)
        x_ref[C : C + 1, :] = x_ref[C : C + 1, :] + x_ref[C + 1 : C + 2, :]
        stage_a_fill(t_a, False)
        h_a = stage_a(t_a, e_a, send_h, recv_h)
        start(h_a)
        arrive(h_a)
        summed = total(t_a[p], e_a)
        t_b[:, :HALF] = summed[:, :HALF].astype(bf16)
        v_high, v_low = split(summed[:, HALF : HALF + 128] + summed[:, HALF + 128 :])
        t_b[:, HALF : HALF + 128] = v_high
        t_b[:, HALF + 128 :] = v_low
        h_b = stage_b(t_b, e_b, send_h, recv_h)
        start(h_b)
        arrive(h_b)
        summed = total(summed, e_b)
        h_buf[pl.ds(own_top, 16), pl.ds(own_left, HALF)] = summed[:, :HALF].astype(bf16)
        h_c = stage_c(h_buf, send_h, recv_h)
        start(h_c)
        put_row(summed[:, HALF : HALF + 128] + summed[:, HALF + 128 :])
        left = lt[...] * (1.0 / math.sqrt(ROWS * SIDE * SIDE))
        l_high, l_low = split(left[:, :C])
        base = left[:, C : C + 1] * vrow[0:1, :]
        arrive(h_c)
        full_h = h_buf[...]
        grads[0] = base + dot(l_high, full_h) + dot(l_low, full_h)
        finish(h_a)
        finish(h_b)
        finish(h_c)


def shards(sn, sc, lv, emb, tim, gain, blk, rdo):
    vmem = pl.BlockSpec(memory_space=pltpu.VMEM)
    scratch = [
        ((C, ROWS), bf16), ((C, ROWS), bf16), ((ROWS // 128, 128), f32), ((1, C, D), bf16),
        ((1, D), f32), ((1, D), f32), ((1, DEPTH, F), bf16), ((1, C, F), bf16),
        ((80, F), f32), ((16, 128), f32), ((8, F), f32),
        ((SIDE, 16, HALF + 128), f32), ((SIDE, 16, HALF + 128), f32),
        ((16, HALF + 128), f32), ((SIDE, 16, HALF + 128), f32),
        ((C, F), f32), ((256, F), bf16),
        ((SIDE, 16, HALF + 256), bf16), ((SIDE, 16, HALF + 256), bf16),
        ((16, HALF + 256), bf16), ((SIDE, 16, HALF + 256), bf16), ((C, F), bf16),
        ((F, 128), bf16), ((256, 128), bf16), ((ROWS, 128), f32), ((ROWS, 128), f32),
        ((ROWS, 256), bf16), ((80, ROWS), bf16), ((ROWS, CHUNK), f32), ((ROWS, 128), f32),
        ((ROWS, F), f32), ((ROWS, F), f32), ((ROWS, 128), f32), ((ROWS, 256), f32),
        ((DEPTH, 128), f32), ((ROWS, 128), f32),
        ((ROWS, 128), f32),
        ((ROWS // 2, 128), bf16), ((ROWS // 2, 128), bf16), ((ROWS // 2, 128), bf16),
        ((4, ROWS // 2, 128), bf16),
    ]
    dma = pltpu.SemaphoreType.DMA
    grads, generated = pl.pallas_call(
        kernel,
        out_shape=(
            jax.ShapeDtypeStruct((1, DEPTH, F), f32),
            jax.ShapeDtypeStruct((C, ROWS), bf16),
        ),
        in_specs=[pl.BlockSpec(memory_space=pltpu.HBM)] * 8,
        out_specs=(vmem, vmem),
        scratch_shapes=[pltpu.VMEM(shape, kind) for shape, kind in scratch]
        + [dma((8,))]
        + [dma((3, SIDE)) for _ in range(4)]
        + [dma((4,)) for _ in range(4)]
        + [pltpu.SemaphoreType.REGULAR],
        compiler_params=pltpu.CompilerParams(
            collective_id=0, has_side_effects=True, vmem_limit_bytes=64 * 2**20
        ),
    )(sn.T, sc.T, lv.reshape(ROWS // 128, 128), emb, tim, gain, blk, rdo.transpose(0, 2, 1))
    return grads, generated.T


def solution(mesh):
    in_specs = (
        P("fsdp", None),
        P("fsdp", None),
        P("fsdp"),
        P("role", None, None),
        P("role", None),
        P("role", None),
        P("role", "fsdp", None),
        P("role", None, None),
    )
    out_specs = (P("role", "fsdp", None), P("fsdp", None))
    return jax.shard_map(shards, mesh=mesh, in_specs=in_specs, out_specs=out_specs, check_vma=False)
```

```python
import functools
import math

import jax
import jax.numpy as jnp
from jax import lax
from jax.experimental import pallas as pl
from jax.experimental.pallas import tpu as pltpu
from jax.sharding import PartitionSpec as P

MESH = pl.DeviceIdType.MESH
f32, bf16 = jnp.float32, jnp.bfloat16
adv_weight = 3.0
ROWS = 384
C = 64
D = 3072
F = 1536
DEPTH = 48
CHUNK = 256
CHUNKS = F // CHUNK
SIDE = 8
HALF = F // 2
YX_ORDER = (5, 3, 4, 7, 1, 6, 2)
Z_ORDER = (4, 5, 3, 6, 2, 7, 1)
ROOT = math.sqrt(2.0 / math.pi)
CUBE = 0.044715 * ROOT


def dot(a, b):
    return jnp.dot(a, b, preferred_element_type=f32)


def dot_nt(a, b):
    return lax.dot_general(a, b, (((1,), (1,)), ((), ())), preferred_element_type=f32)


def split(value):
    high = value.astype(bf16)
    return high, (value - high.astype(f32)).astype(bf16)


def lanes(shape):
    return lax.broadcasted_iota(jnp.int32, shape, len(shape) - 1)


def pack(value):
    top, bottom = value[: ROWS // 2], value[ROWS // 2 :]
    return jnp.where(lanes(top.shape) < C, top, bottom)


def unpack(value):
    turned = pltpu.roll(value, C, 1)
    left = lanes(value.shape) < C
    return jnp.concatenate([jnp.where(left, value, turned), jnp.where(left, turned, value)], axis=0)


def gelu_parts(hidden):
    square = hidden * hidden
    half = 0.5 + 0.5 * jnp.tanh(hidden * (ROOT + CUBE * square))
    return square, half, hidden * half


def gelu_slope(square, half, value):
    return half + value * (1.0 - half) * (2.0 * ROOT + 6.0 * CUBE * square)


def kernel(
    *refs,
):
    hbm, (grads, gen_out), scratch, (fetch, *sems) = refs[:8], refs[8:10], refs[10:-10], refs[-10:]
    step(hbm, fetch, grads, gen_out, *scratch, *sems)


def step(
    hbm, fetch, grads, gen_out,
    sn, sc, lv, emb, tim, gain, blk, rdo, x_ref, vt, vrow, s_a, d_a, s_b, d_b, m_buf, m_aug,
    t_a, e_a, t_b, e_b, h_buf,
    r2, gram, level, z_f32, z_aug, z_t, rs, y_ref, hid, slope, acc, back_acc, lt, cot,
    noise_in, gen_pk, gen_in, out_pk, col_in,
    send_m, recv_m, send_h, recv_h, send_g, recv_g, send_c, recv_c, turn,
):
    role = lax.axis_index("role")
    place = lax.axis_index("fsdp")
    p, z = place // SIDE, place % SIDE

    def yx_peer(k):
        return (role, lax.rem(p + k, SIDE) * SIDE + z)

    def z_peer(k):
        return (role, p * SIDE + lax.rem(z + k, SIDE))

    def role_peer(k):
        return (lax.rem(role + k, 4), place)

    barrier = pltpu.get_barrier_semaphore()
    for k_yx, k_z in zip(YX_ORDER, Z_ORDER):
        pl.semaphore_signal(barrier, inc=1, device_id=yx_peer(k_yx), device_id_type=MESH)
        pl.semaphore_signal(barrier, inc=1, device_id=z_peer(k_z), device_id_type=MESH)
    for k in range(1, 4):
        pl.semaphore_signal(barrier, inc=1, device_id=role_peer(k), device_id_type=MESH)

    fetches = [
        pltpu.make_async_copy(src, dst, fetch.at[i])
        for i, (src, dst) in enumerate(zip(hbm, (sn, sc, lv, emb, tim, gain, blk, rdo)))
    ]
    for i in (4, 5, 3, 6, 7, 0, 1, 2):
        fetches[i].start()

    def remote(src, dst, send, recv, device):
        return pltpu.make_async_remote_copy(
            src_ref=src, dst_ref=dst, send_sem=send, recv_sem=recv, device_id=device,
            device_id_type=MESH,
        )

    begin = place * DEPTH
    window = jnp.minimum(begin // 128, D // 128 - 2) * 128
    window = pl.multiple_of(window, 128)
    wide = pl.ds(window, 256)
    for i in (4, 5, 3, 6):
        fetches[i].wait()
    gain_w = gain[:, wide]
    lifted = jnp.concatenate(
        [
            emb[0, :, wide].astype(f32) * gain_w,
            jnp.where(
                lax.broadcasted_iota(jnp.int32, (16, 256), 0) == 0, tim[:, wide] * gain_w, 0.0
            ),
        ],
        axis=0,
    )
    lifted = pltpu.roll(lifted, lax.rem(256 + window - begin, 256), 1)[:, :128]
    high, low = split(lifted[:, :DEPTH])
    block = blk[0]
    x_ref[...] = dot(high, block) + dot(low, block)

    def stage_a_fill(send, wide_type):
        vt[...] = jnp.zeros_like(vt)
        for i in range(F // 128):
            vt[i : i + 1, :] = x_ref[C : C + 1, i * 128 : i * 128 + 128]
        tile = vt[...]
        for piece in range(SIDE):
            top, left = piece // 2 * 16, piece % 2 * HALF
            part = x_ref[top : top + 16, left : left + HALF]
            if wide_type:
                send[piece, :, :HALF] = part
                send[piece, :, HALF:] = tile
            else:
                send[piece, :, :HALF] = part.astype(bf16)
                v_high, v_low = split(tile)
                send[piece, :, HALF : HALF + 128] = v_high
                send[piece, :, HALF + 128 :] = v_low

    def stage_a(send, dest, ss, rr):
        return [
            remote(send.at[lax.rem(p + k, SIDE)], dest.at[k], ss.at[0, k], rr.at[0, k], yx_peer(k))
            for k in YX_ORDER
        ]

    def stage_b(send, dest, ss, rr):
        return [
            remote(send, dest.at[k], ss.at[1, k], rr.at[1, k], z_peer(k)) for k in Z_ORDER
        ]

    own_top = pl.multiple_of(p // 2 * 16, 16)
    own_left = pl.multiple_of(lax.rem(p, 2) * HALF, 128)

    def stage_c(buf, ss, rr):
        own = buf.at[pl.ds(own_top, 16), pl.ds(own_left, HALF)]
        return [remote(own, own, ss.at[2, k], rr.at[2, k], yx_peer(k)) for k in YX_ORDER]

    def start(copies):
        for copy in copies:
            copy.start()

    def arrive(copies):
        for copy in copies:
            copy.wait_recv()

    def finish(copies):
        for copy in copies:
            copy.wait_send()

    def total(first, dest):
        value = first.astype(f32)
        for k in range(1, SIDE):
            value = value + dest[k].astype(f32)
        return value

    def put_row(tile):
        vt[...] = tile
        for i in range(F // 128):
            vrow[0:1, i * 128 : i * 128 + 128] = vt[i : i + 1, :]

    stage_a_fill(s_a, False)
    pl.semaphore_wait(barrier, 2 * (SIDE - 1) + 3)
    m_a = stage_a(s_a, d_a, send_m, recv_m)

    @pl.when((role == 1) | (role == 2))
    def _():
        pl.semaphore_wait(turn, 1)

    start(m_a)

    for i in (0, 1, 2, 7):
        fetches[i].wait()

    lt[...] = jnp.concatenate([lifted, jnp.zeros((48, 128), f32)], axis=0).T[:DEPTH]
    for i in range(ROWS // 128):
        level[i * 128 : i * 128 + 128, :] = jnp.broadcast_to(lv[i : i + 1, :], (128, 128)).T
    readout = rdo[0].astype(f32)
    r2[...] = jnp.concatenate([readout, readout], axis=0).T.astype(bf16)
    time = tim[...]
    t_1 = time.astype(bf16).astype(f32)
    t_2 = (time - t_1).astype(bf16).astype(f32)
    t_3 = time - t_1 - t_2
    rows = lax.broadcasted_iota(jnp.int32, (16, D), 0)
    parts = jnp.where(rows == 0, t_1, jnp.where(rows == 1, t_2, jnp.where(rows == 2, t_3, 0.0)))
    square_e = dot_nt(emb[0], emb[0])
    cross = jnp.sum(dot_nt(parts.astype(bf16), emb[0]), axis=0, keepdims=True)
    square_e = jnp.concatenate([square_e, square_e], axis=1)
    cross = jnp.concatenate([cross, cross], axis=1)
    square_t = jnp.sum(time * time, axis=1, keepdims=True)
    g_1, rest = split(square_e)
    rest = square_e - g_1.astype(f32)
    g_2, g_3 = split(rest)
    gram[0:64, :] = g_1
    gram[64:128, :] = g_2
    gram[128:192, :] = g_3
    gram[192:256, :] = jnp.zeros((64, 128), bf16)

    def rows_in(latent, lev):
        lane = lanes((ROWS, 128))
        lev_high = lev.astype(bf16).astype(f32)
        lev_low = lev - lev_high
        z_f32[...] = latent
        latent16 = latent.astype(bf16)
        z_aug[:, :128] = latent16
        z_aug[:, 128:] = jnp.where(
            lane < 2, lev_high, jnp.where(lane == 2, lev_low, 0.0)
        ).astype(bf16)
        y = (
            dot(latent16, gram[0:128, :]) + dot(latent16, gram[128:256, :]) + lev * cross
        )
        y_ref[...] = y
        mean = (
            0.5 * jnp.sum(latent * (y + lev * cross), axis=1, keepdims=True)
            + lev[:, :1] * lev[:, :1] * square_t
        ) * (1.0 / D)
        rs[...] = jnp.broadcast_to(lax.rsqrt(jnp.maximum(mean, 0.0) + 1e-06), (ROWS, CHUNK))

    def rows_turned():
        lane = lanes((ROWS, 128))
        lev = jnp.where(role == 0, 1.0, level[...])
        lev_high = lev.astype(bf16).astype(f32)
        lev_low = lev - lev_high
        turned = jnp.where(
            lane < C, z_f32[...], jnp.where(lane == C, lev_high, jnp.where(lane == C + 1, lev_low, 0.0))
        ).T
        z_t[...] = turned[:80].astype(bf16)

    arrive(m_a)

    @pl.when((role == 0) | (role == 3))
    def _():
        pl.semaphore_signal(
            turn, inc=1, device_id=(jnp.where(role == 0, 1, 2), place), device_id_type=MESH
        )

    summed = total(s_a[p], d_a)
    s_b[:, :HALF] = summed[:, :HALF].astype(bf16)
    v_high, v_low = split(summed[:, HALF : HALF + 128] + summed[:, HALF + 128 :])
    s_b[:, HALF : HALF + 128] = v_high
    s_b[:, HALF + 128 :] = v_low
    m_b = stage_b(s_b, d_b, send_m, recv_m)
    start(m_b)
    m_aug[128 + 16 :, :] = jnp.zeros((128 - 16, F), bf16)

    @pl.when(role == 0)
    def _():
        noise = sn[...].astype(f32)
        rows_in(jnp.concatenate([noise, noise], axis=0).T, jnp.ones((ROWS, 128), f32))

    @pl.when(role != 0)
    def _():
        noise = sc[...].astype(f32)
        noise_in[...] = level[...] * jnp.concatenate([noise, noise], axis=0).T

    arrive(m_b)
    summed = total(summed, d_b)
    m_buf[pl.ds(own_top, 16), pl.ds(own_left, HALF)] = summed[:, :HALF].astype(bf16)
    m_c = stage_c(m_buf, send_m, recv_m)
    start(m_c)
    put_row(summed[:, HALF : HALF + 128] + summed[:, HALF + 128 :])
    v_full = vrow[0:1, :]
    v_high = v_full.astype(bf16).astype(f32)
    rows = lax.broadcasted_iota(jnp.int32, (16, F), 0)
    m_aug[128:144, :] = jnp.where(
        (rows == 0) | (rows == 2), v_high, jnp.where(rows == 1, v_full - v_high, 0.0)
    ).astype(bf16)
    arrive(m_c)
    m_aug[0:64, :] = m_buf[...]
    m_aug[64:128, :] = jnp.zeros((64, F), bf16)
    finish(m_a)
    finish(m_b)
    finish(m_c)

    def columns(c):
        return pl.ds(pl.multiple_of(c * CHUNK, CHUNK), CHUNK)

    def forward(critic):
        acc[...] = jnp.zeros_like(acc)
        if critic:
            back_acc[...] = jnp.zeros_like(back_acc)

        def body(c, carry):
            cs = columns(c)
            hidden = dot(z_aug[...], m_aug[:, cs]) * rs[...]
            square, half, value = gelu_parts(hidden)
            acc[...] += dot(value.astype(bf16), r2[cs, :])
            if critic:
                rise = gelu_slope(square, half, value)
                slope[:, cs] = rise * rs[...]
                weight = dot(jnp.ones((16, C), bf16), rdo[0, :, cs])[0:1, :]
                back_acc[...] += dot_nt((rise * weight).astype(bf16), m_aug[:, cs])
            else:
                hid[:, cs] = hidden
            return carry

        lax.fori_loop(0, CHUNKS, body, 0, unroll=6)
        return acc[...].astype(bf16).astype(f32)

    def slopes():
        def body(c, carry):
            cs = columns(c)
            slope[:, cs] = gelu_slope(*gelu_parts(hid[:, cs])) * rs[...]
            return carry

        lax.fori_loop(0, CHUNKS, body, 0, unroll=6)

    to_gen = (0, place)

    @pl.when(role == 0)
    def _():
        out = forward(False)
        gen_pk[...] = pack(out).astype(bf16)
        copies = [
            remote(gen_pk, gen_in, send_g.at[k], recv_g.at[0], (k, place)) for k in range(1, 4)
        ]
        start(copies)
        gen_out[...] = out.T[:C].astype(bf16)
        slopes()
        rows_turned()
        finish(copies)
        sources = [
            remote(out_pk, col_in.at[k], send_c.at[0], recv_c.at[k], (k, place))
            for k in range(1, 4)
        ]
        arrive(sources)
        real = unpack(col_in[1].astype(f32))
        fake = unpack(col_in[2].astype(f32))
        adversarial = unpack(col_in[3].astype(f32))
        spread = jnp.sum(jnp.abs(out - real), axis=1, keepdims=True) * (0.5 / C) + 1e-05
        dmd = ((fake - real) / spread).astype(bf16).astype(f32)
        cot[...] = dmd + adversarial

    @pl.when(role != 0)
    def _():
        remote(gen_pk, gen_in, send_g.at[0], recv_g.at[0], to_gen).wait_recv()
        gen32 = unpack(gen_in[...].astype(f32))
        lev = level[...]
        noised = (1.0 - lev) * gen32 + noise_in[...]
        rows_in(noised.astype(bf16).astype(f32), lev)

        def deliver(value):
            out_pk[...] = pack(value).astype(bf16)
            copy = remote(out_pk, col_in.at[role], send_c.at[0], recv_c.at[role], to_gen)
            copy.start()
            return copy

        @pl.when(role == 3)
        def _():
            out = forward(True)
            logit = 0.5 * jnp.sum(out, axis=1, keepdims=True)
            down = -1.0 / (1.0 + jnp.exp(logit))
            through = back_acc[...]
            pulled = jnp.sum(z_aug[...].astype(f32) * through, axis=1, keepdims=True)
            latent = through[:, :128]
            latent = latent + pltpu.roll(latent, C, 1)
            inverse = rs[:, :128]
            back = inverse * latent - inverse * inverse * inverse * (1.0 / D) * pulled * y_ref[...]
            copy = deliver(adv_weight * (1.0 - level[...]) * down * back)
            gen_out[...] = gen32.T[:C].astype(bf16)
            cot[...] = jnp.broadcast_to(1.0 / (1.0 + jnp.exp(-logit)), (ROWS, 128))
            rows_turned()
            copy.wait_send()

        @pl.when(role != 3)
        def _():
            out = forward(False)
            copy = deliver(out)
            gen_out[...] = gen32.T[:C].astype(bf16)
            cot[...] = out - gen32

            @pl.when(role == 2)
            def _():
                slopes()
                rows_turned()

            copy.wait_send()

    @pl.when(role == 1)
    def _():
        grads[...] = jnp.zeros_like(grads)

    @pl.when(role != 1)
    def _():
        lane = lanes((ROWS, 128))
        full = cot[...]
        c_high = full.astype(bf16).astype(f32)
        cot2 = jnp.where(lane < C, c_high, full - c_high).astype(bf16)

        def body(c, carry):
            cs = columns(c)
            hcot = (dot_nt(cot2, r2[cs, :]) * slope[:, cs]).astype(bf16)
            x_ref[:, cs] = dot(z_t[...], hcot)
            return carry

        lax.fori_loop(0, CHUNKS, body, 0, unroll=6)
        x_ref[C : C + 1, :] = x_ref[C : C + 1, :] + x_ref[C + 1 : C + 2, :]
        stage_a_fill(t_a, False)
        h_a = stage_a(t_a, e_a, send_h, recv_h)
        start(h_a)
        arrive(h_a)
        summed = total(t_a[p], e_a)
        t_b[:, :HALF] = summed[:, :HALF].astype(bf16)
        v_high, v_low = split(summed[:, HALF : HALF + 128] + summed[:, HALF + 128 :])
        t_b[:, HALF : HALF + 128] = v_high
        t_b[:, HALF + 128 :] = v_low
        h_b = stage_b(t_b, e_b, send_h, recv_h)
        start(h_b)
        arrive(h_b)
        summed = total(summed, e_b)
        h_buf[pl.ds(own_top, 16), pl.ds(own_left, HALF)] = summed[:, :HALF].astype(bf16)
        h_c = stage_c(h_buf, send_h, recv_h)
        start(h_c)
        put_row(summed[:, HALF : HALF + 128] + summed[:, HALF + 128 :])
        left = lt[...] * (1.0 / math.sqrt(ROWS * SIDE * SIDE))
        l_high, l_low = split(left[:, :C])
        base = left[:, C : C + 1] * vrow[0:1, :]
        arrive(h_c)
        full_h = h_buf[...]
        grads[0] = base + dot(l_high, full_h) + dot(l_low, full_h)
        finish(h_a)
        finish(h_b)
        finish(h_c)


def shards(sn, sc, lv, emb, tim, gain, blk, rdo):
    vmem = pl.BlockSpec(memory_space=pltpu.VMEM)
    scratch = [
        ((C, ROWS), bf16), ((C, ROWS), bf16), ((ROWS // 128, 128), f32), ((1, C, D), bf16),
        ((1, D), f32), ((1, D), f32), ((1, DEPTH, F), bf16), ((1, C, F), bf16),
        ((80, F), f32), ((16, 128), f32), ((8, F), f32),
        ((SIDE, 16, HALF + 256), bf16), ((SIDE, 16, HALF + 256), bf16),
        ((16, HALF + 256), bf16), ((SIDE, 16, HALF + 256), bf16),
        ((C, F), bf16), ((256, F), bf16),
        ((SIDE, 16, HALF + 256), bf16), ((SIDE, 16, HALF + 256), bf16),
        ((16, HALF + 256), bf16), ((SIDE, 16, HALF + 256), bf16), ((C, F), bf16),
        ((F, 128), bf16), ((256, 128), bf16), ((ROWS, 128), f32), ((ROWS, 128), f32),
        ((ROWS, 256), bf16), ((80, ROWS), bf16), ((ROWS, CHUNK), f32), ((ROWS, 128), f32),
        ((ROWS, F), f32), ((ROWS, F), f32), ((ROWS, 128), f32), ((ROWS, 256), f32),
        ((DEPTH, 128), f32), ((ROWS, 128), f32),
        ((ROWS, 128), f32),
        ((ROWS // 2, 128), bf16), ((ROWS // 2, 128), bf16), ((ROWS // 2, 128), bf16),
        ((4, ROWS // 2, 128), bf16),
    ]
    dma = pltpu.SemaphoreType.DMA
    grads, generated = pl.pallas_call(
        kernel,
        out_shape=(
            jax.ShapeDtypeStruct((1, DEPTH, F), f32),
            jax.ShapeDtypeStruct((C, ROWS), bf16),
        ),
        in_specs=[pl.BlockSpec(memory_space=pltpu.HBM)] * 8,
        out_specs=(vmem, vmem),
        scratch_shapes=[pltpu.VMEM(shape, kind) for shape, kind in scratch]
        + [dma((8,))]
        + [dma((3, SIDE)) for _ in range(4)]
        + [dma((4,)) for _ in range(4)]
        + [pltpu.SemaphoreType.REGULAR],
        compiler_params=pltpu.CompilerParams(
            collective_id=0, has_side_effects=True, vmem_limit_bytes=32 * 2**20
        ),
    )(
        *(
            pltpu.with_memory_space_constraint(array, pltpu.HBM)
            for array in (
                sn.T, sc.T, lv.reshape(ROWS // 128, 128), emb, tim, gain, blk,
                rdo.transpose(0, 2, 1),
            )
        )
    )
    return grads, generated.T


def solution(mesh):
    in_specs = (
        P("fsdp", None),
        P("fsdp", None),
        P("fsdp"),
        P("role", None, None),
        P("role", None),
        P("role", None),
        P("role", "fsdp", None),
        P("role", None, None),
    )
    out_specs = (P("role", "fsdp", None), P("fsdp", None))
    return jax.shard_map(shards, mesh=mesh, in_specs=in_specs, out_specs=out_specs, check_vma=False)
```

```python
import functools
import math

import jax
import jax.numpy as jnp
from jax import lax
from jax.experimental import pallas as pl
from jax.experimental.pallas import tpu as pltpu
from jax.sharding import PartitionSpec as P

MESH = pl.DeviceIdType.MESH
f32, bf16 = jnp.float32, jnp.bfloat16
adv_weight = 3.0
ROWS = 384
C = 64
D = 3072
F = 1536
DEPTH = 48
CHUNK = 256
CHUNKS = F // CHUNK
SIDE = 8
HALF = F // 2
YX_ORDER = (5, 3, 4, 7, 1, 6, 2)
Z_ORDER = (4, 5, 3, 6, 2, 7, 1)
ROOT = math.sqrt(2.0 / math.pi)
CUBE = 0.044715 * ROOT


def dot(a, b):
    return jnp.dot(a, b, preferred_element_type=f32)


def dot_nt(a, b):
    return lax.dot_general(a, b, (((1,), (1,)), ((), ())), preferred_element_type=f32)


def split(value):
    high = value.astype(bf16)
    return high, (value - high.astype(f32)).astype(bf16)


def lanes(shape):
    return lax.broadcasted_iota(jnp.int32, shape, len(shape) - 1)


def pack(value):
    top, bottom = value[: ROWS // 2], value[ROWS // 2 :]
    return jnp.where(lanes(top.shape) < C, top, bottom)


def unpack(value):
    turned = pltpu.roll(value, C, 1)
    left = lanes(value.shape) < C
    return jnp.concatenate([jnp.where(left, value, turned), jnp.where(left, turned, value)], axis=0)


def gelu_parts(hidden):
    square = hidden * hidden
    half = 0.5 + 0.5 * jnp.tanh(hidden * (ROOT + CUBE * square))
    return square, half, hidden * half


def gelu_slope(square, half, value):
    return half + value * (1.0 - half) * (2.0 * ROOT + 6.0 * CUBE * square)


def kernel(
    *refs,
):
    hbm, (grads, gen_out), scratch, (fetch, *sems) = refs[:8], refs[8:10], refs[10:-12], refs[-12:]
    step(hbm, fetch, grads, gen_out, *scratch, *sems)


def step(
    hbm, fetch, grads, gen_out,
    sn, sc, lv, emb, tim, gain, blk, rdo, x_ref, vt, vrow, s_a, d_a, s_b, d_b, m_all, rsum, gen_f, rd_in, rs_row, rs_in,
    t_a, e_a, t_b, e_b, h_buf,
    r2_all, gram, level, z_f32, z_all, z_t, rs_all, y_ref, hid, slope, lt, cot,
    noise_in, gen_pk, gen_in, out_pk, col_in,
    send_m, recv_m, send_h, recv_h, send_g, recv_g, send_c, recv_c, send_x, recv_x, turn,
):
    role = lax.axis_index("role")
    place = lax.axis_index("fsdp")
    p, z = place // SIDE, place % SIDE
    slot = jnp.where(role == 0, 0, 1)

    def yx_peer(k):
        return (role, lax.rem(p + k, SIDE) * SIDE + z)

    def z_peer(k):
        return (role, p * SIDE + lax.rem(z + k, SIDE))

    def role_peer(k):
        return (lax.rem(role + k, 4), place)

    barrier = pltpu.get_barrier_semaphore()
    for k_yx, k_z in zip(YX_ORDER, Z_ORDER):
        pl.semaphore_signal(barrier, inc=1, device_id=yx_peer(k_yx), device_id_type=MESH)
        pl.semaphore_signal(barrier, inc=1, device_id=z_peer(k_z), device_id_type=MESH)
    for k in range(1, 4):
        pl.semaphore_signal(barrier, inc=1, device_id=role_peer(k), device_id_type=MESH)

    fetches = [
        pltpu.make_async_copy(src, dst, fetch.at[i])
        for i, (src, dst) in enumerate(zip(hbm, (sn, sc, lv, emb, tim, gain, blk, rdo)))
    ]
    for i in (4, 5, 3, 6, 7, 0, 1, 2):
        fetches[i].start()

    def remote(src, dst, send, recv, device):
        return pltpu.make_async_remote_copy(
            src_ref=src, dst_ref=dst, send_sem=send, recv_sem=recv, device_id=device,
            device_id_type=MESH,
        )

    begin = place * DEPTH
    window = jnp.minimum(begin // 128, D // 128 - 2) * 128
    window = pl.multiple_of(window, 128)
    wide = pl.ds(window, 256)
    for i in (4, 5, 3, 6):
        fetches[i].wait()
    gain_w = gain[:, wide]
    lifted = jnp.concatenate(
        [
            emb[0, :, wide].astype(f32) * gain_w,
            jnp.where(
                lax.broadcasted_iota(jnp.int32, (16, 256), 0) == 0, tim[:, wide] * gain_w, 0.0
            ),
        ],
        axis=0,
    )
    lifted = pltpu.roll(lifted, lax.rem(256 + window - begin, 256), 1)[:, :128]
    high, low = split(lifted[:, :DEPTH])
    block = blk[0]
    x_ref[...] = dot(high, block) + dot(low, block)

    def stage_a_fill(send, low_too):
        vt[...] = jnp.zeros_like(vt)
        for i in range(F // 128):
            vt[i : i + 1, :] = x_ref[C : C + 1, i * 128 : i * 128 + 128]
        tile = vt[...]
        for piece in range(SIDE):
            top, left = piece // 2 * 16, piece % 2 * HALF
            send[piece, :, :HALF] = x_ref[top : top + 16, left : left + HALF].astype(bf16)
            v_high, v_low = split(tile)
            send[piece, :, HALF : HALF + 128] = v_high
            if low_too:
                send[piece, :, HALF + 128 :] = v_low

    def stage_a(send, dest, ss, rr):
        return [
            remote(send.at[lax.rem(p + k, SIDE)], dest.at[k], ss.at[0, k], rr.at[0, k], yx_peer(k))
            for k in YX_ORDER
        ]

    def stage_b(send, dest, ss, rr):
        return [
            remote(send, dest.at[k], ss.at[1, k], rr.at[1, k], z_peer(k)) for k in Z_ORDER
        ]

    own_top = pl.multiple_of(p // 2 * 16, 16)
    own_left = pl.multiple_of(lax.rem(p, 2) * HALF, 128)

    other_left = pl.multiple_of(HALF - own_left, 128)
    own_block = (pl.ds(own_top, 16), pl.ds(own_left, HALF))

    def stage_c(buf, ss, rr):
        own = buf.at[own_block]
        return [remote(own, own, ss.at[2, k], rr.at[2, k], yx_peer(k)) for k in YX_ORDER]

    def start(copies):
        for copy in copies:
            copy.start()

    def arrive(copies):
        for copy in copies:
            copy.wait_recv()

    def finish(copies):
        for copy in copies:
            copy.wait_send()

    def total(first, dest):
        value = first.astype(f32)
        for k in range(1, SIDE):
            value = value + dest[k].astype(f32)
        return value

    def put_row(tile):
        vt[...] = tile
        for i in range(F // 128):
            vrow[0:1, i * 128 : i * 128 + 128] = vt[i : i + 1, :]

    stage_a_fill(s_a, True)
    pl.semaphore_wait(barrier, 2 * (SIDE - 1) + 3)
    m_a = stage_a(s_a, d_a, send_m, recv_m)

    @pl.when(role == 1)
    def _():
        pl.semaphore_wait(turn, 1)

    start(m_a)

    for i in (0, 1, 2, 7):
        fetches[i].wait()

    lt[...] = jnp.concatenate([lifted, jnp.zeros((48, 128), f32)], axis=0).T[:DEPTH]
    for i in range(ROWS // 128):
        level[i * 128 : i * 128 + 128, :] = jnp.broadcast_to(lv[i : i + 1, :], (128, 128)).T
    readout = rdo[0].astype(f32)
    rsum[...] = dot(jnp.ones((16, C), bf16), rdo[0])[:8]
    r2_all[slot] = jnp.concatenate([readout, readout], axis=0).T.astype(bf16)
    time = tim[...]
    t_1 = time.astype(bf16).astype(f32)
    t_2 = (time - t_1).astype(bf16).astype(f32)
    t_3 = time - t_1 - t_2
    rows = lax.broadcasted_iota(jnp.int32, (16, D), 0)
    parts = jnp.where(rows == 0, t_1, jnp.where(rows == 1, t_2, jnp.where(rows == 2, t_3, 0.0)))
    square_e = dot_nt(emb[0], emb[0])
    cross = jnp.sum(dot_nt(parts.astype(bf16), emb[0]), axis=0, keepdims=True)
    square_e = jnp.concatenate([square_e, square_e], axis=1)
    cross = jnp.concatenate([cross, cross], axis=1)
    square_t = jnp.sum(time * time, axis=1, keepdims=True)
    g_1, rest = split(square_e)
    rest = square_e - g_1.astype(f32)
    g_2, g_3 = split(rest)
    for i, part in enumerate((g_1, g_2, g_3)):
        gram[i, :C] = part
        gram[i, C:] = jnp.zeros((C, 128), bf16)
    m_all[0, 80:, :] = jnp.zeros((48, F), bf16)
    m_all[1, 80:, :] = jnp.zeros((48, F), bf16)

    def rows_with(latent, lev):
        lane = lanes((ROWS, 128))
        lev_high = lev.astype(bf16).astype(f32)
        return jnp.where(
            lane < C,
            latent,
            jnp.where(lane < C + 2, lev_high, jnp.where(lane == C + 2, lev - lev_high, 0.0)),
        ).astype(bf16)

    def rows_in(to, latent, lev):
        z_f32[...] = latent
        z16 = rows_with(latent, lev)
        z_all[to] = z16
        y = dot(z16, gram[0]) + dot(z16, gram[1]) + dot(z16, gram[2]) + lev * cross
        y_ref[...] = y
        mean = (
            0.5 * jnp.sum(latent * (y + lev * cross), axis=1, keepdims=True)
            + lev[:, :1] * lev[:, :1] * square_t
        ) * (1.0 / D)
        rs_all[to] = jnp.broadcast_to(lax.rsqrt(jnp.maximum(mean, 0.0) + 1e-06), (ROWS, CHUNK))

    def rows_turned():
        lane = lanes((ROWS, 128))
        lev = jnp.where(role == 0, 1.0, level[...])
        lev_high = lev.astype(bf16).astype(f32)
        turned = jnp.where(
            lane < C,
            z_f32[...],
            jnp.where(lane == C, lev_high, jnp.where(lane == C + 1, lev - lev_high, 0.0)),
        ).T
        z_t[...] = turned[:80].astype(bf16)

    critic_here = (3, place)
    x_readout = remote(rdo.at[0], rd_in, send_x.at[8], recv_x.at[8], critic_here)
    x_scales = remote(rs_row, rs_in, send_x.at[9], recv_x.at[9], critic_here)
    level_rows = m_all.at[0, pl.ds(C, 16), :]
    x_level = remote(level_rows, level_rows, send_x.at[10], recv_x.at[10], critic_here)
    matrix_block = m_all.at[(0, *own_block)]
    x_matrix = {
        k: remote(
            matrix_block, matrix_block, send_x.at[k], recv_x.at[k],
            (3, lax.rem(p + k, SIDE) * SIDE + z),
        )
        for k in (*YX_ORDER, 0)
    }

    arrive(m_a)

    @pl.when(role == 0)
    def _():
        pl.semaphore_signal(
            turn, inc=1, device_id=(jnp.where(role == 0, 1, 2), place), device_id_type=MESH
        )

    summed = total(s_a[p], d_a)
    s_b[:, :HALF] = summed[:, :HALF].astype(bf16)
    v_high, v_low = split(summed[:, HALF : HALF + 128] + summed[:, HALF + 128 :])
    s_b[:, HALF : HALF + 128] = v_high
    s_b[:, HALF + 128 :] = v_low
    m_b = stage_b(s_b, d_b, send_m, recv_m)
    start(m_b)

    @pl.when((role == 0) | (role == 3))
    def _():
        noise = sn[...].astype(f32)
        noise = jnp.concatenate([noise, noise], axis=0).T

        @pl.when(role == 0)
        def _():
            x_readout.start()
            rows_in(0, noise, jnp.ones((ROWS, 128), f32))
            rs_row[...] = rs_all[0, :, :128].T[:8]
            x_scales.start()

        @pl.when(role == 3)
        def _():
            z_all[0] = rows_with(noise, jnp.ones((ROWS, 128), f32))

    @pl.when(role != 0)
    def _():
        noise = sc[...].astype(f32)
        noise_in[...] = level[...] * jnp.concatenate([noise, noise], axis=0).T

    arrive(m_b)
    summed = total(summed, d_b)
    m_all[(slot, *own_block)] = summed[:, :HALF].astype(bf16)
    m_c = dict(zip(YX_ORDER, stage_c(m_all.at[slot], send_m, recv_m)))
    for k in YX_ORDER:
        m_c[k].start()

        @pl.when(role == 0)
        def _():
            x_matrix[k].start()

    put_row(summed[:, HALF : HALF + 128] + summed[:, HALF + 128 :])
    v_full = vrow[0:1, :]
    v_high = v_full.astype(bf16).astype(f32)
    rows = lax.broadcasted_iota(jnp.int32, (16, F), 0)
    m_all[slot, C : C + 16, :] = jnp.where(
        (rows == 0) | (rows == 2), v_high, jnp.where(rows == 1, v_full - v_high, 0.0)
    ).astype(bf16)

    @pl.when(role == 0)
    def _():
        x_level.start()
        x_matrix[0].start()

    near, far = (2, 4, 6), (1, 3, 5, 7)

    @pl.when(role != 0)
    def _():
        arrive(m_c.values())

    @pl.when(role == 3)
    def _():
        x_readout.wait_recv()
        first = rd_in[...].astype(f32)
        r2_all[0] = jnp.concatenate([first, first], axis=0).T.astype(bf16)
        x_scales.wait_recv()
        for i in range(ROWS // 128):
            here = slice(i * 128, i * 128 + 128)
            scales = jnp.broadcast_to(rs_in[0:1, here], (128, 128)).T
            rs_all[0, here, :128] = scales
            rs_all[0, here, 128:] = scales
        x_level.wait_recv()

    def columns(c):
        left = own_left if c < CHUNKS // 2 else other_left
        return pl.ds(pl.multiple_of(left + c % (CHUNKS // 2) * CHUNK, CHUNK), CHUNK)

    def forward(net, critic, before=None):
        out = jnp.zeros((ROWS, 128), f32)
        through = jnp.zeros((ROWS, 128), f32)
        for c in range(CHUNKS):
            if before and c % (CHUNKS // 2) == 0:
                before(c)
            cs = columns(c)
            hidden = dot(z_all[net], m_all[net, :, cs]) * rs_all[net]
            square, half, value = gelu_parts(hidden)
            out += dot(value.astype(bf16), r2_all[net, cs, :])
            if critic:
                rise = gelu_slope(square, half, value)
                slope[:, cs] = rise * rs_all[net]
                through += dot_nt((rise * rsum[0:1, cs]).astype(bf16), m_all[net, :, cs])
            else:
                hid[:, cs] = hidden
        return out.astype(bf16).astype(f32), through

    def slopes():
        for c in range(CHUNKS):
            cs = pl.ds(c * CHUNK, CHUNK)
            slope[:, cs] = gelu_slope(*gelu_parts(hid[:, cs])) * rs_all[slot]

    hand_on = remote(
        gen_pk, gen_in, send_g.at[0], recv_g.at[0], (jnp.where(role == 0, 1, 2), place)
    )

    def to_gen(source, device):
        return remote(
            out_pk, col_in.at[source], send_c.at[0], recv_c.at[source], (device, place)
        )

    @pl.when((role == 0) | (role == 3))
    def _():
        def matrix_in(c):
            @pl.when(role == 0)
            def _():
                arrive([m_c[k] for k in (near if c == 0 else far)])

            @pl.when(role == 3)
            def _():
                arrive([x_matrix[k] for k in ((0, *near) if c == 0 else far)])

        out, unused = forward(0, False, matrix_in)
        gen_f[...] = out
        gen_pk[...] = pack(out).astype(bf16)
        hand_on.start()

    @pl.when(role == 0)
    def _():
        gen_out[...] = gen_f[...].T[:C].astype(bf16)
        slopes()
        rows_turned()
        finish(x_matrix.values())
        finish((x_readout, x_scales, x_level, hand_on))

    @pl.when(role != 0)
    def _():
        @pl.when(role != 3)
        def _():
            hand_on.wait_recv()
            gen_f[...] = unpack(gen_in[...].astype(f32))

        lev = level[...]
        noised = (1.0 - lev) * gen_f[...] + noise_in[...]
        rows_in(1, noised.astype(bf16).astype(f32), lev)

        @pl.when(role == 3)
        def _():
            out, through = forward(1, True)
            logit = 0.5 * jnp.sum(out, axis=1, keepdims=True)
            down = -1.0 / (1.0 + jnp.exp(logit))
            pulled = jnp.sum(z_all[1].astype(f32) * through, axis=1, keepdims=True)
            latent = jnp.where(lanes((ROWS, 128)) < C, through, pltpu.roll(through, C, 1))
            inverse = rs_all[1, :, :128]
            back = inverse * (latent - inverse * inverse * (1.0 / D) * pulled * y_ref[...])
            out_pk[...] = pack(adv_weight * (1.0 - lev) * down * back).astype(bf16)
            to_gen(3, 0).start()
            cot[...] = jnp.broadcast_to(1.0 / (1.0 + jnp.exp(-logit)), (ROWS, 128))
            hand_on.wait_send()

        @pl.when(role != 3)
        def _():
            out, unused = forward(1, False)
            out_pk[...] = pack(out).astype(bf16)
            to_gen(role, 0).start()
            cot[...] = out - gen_f[...]

        @pl.when(role == 2)
        def _():
            slopes()

        rows_turned()
        gen_out[...] = gen_f[...].T[:C].astype(bf16)
        to_gen(role, 0).wait_send()

    finish(m_a)
    finish(m_b)
    finish(m_c.values())

    @pl.when(role == 1)
    def _():
        grads[...] = jnp.zeros_like(grads)

    @pl.when(role == 0)
    def _():
        for source in (1, 2, 3):
            to_gen(source, source).wait_recv()
        real, fake, adversarial = [unpack(col_in[k].astype(f32)) for k in (1, 2, 3)]
        gen32 = gen_f[...]
        spread = jnp.sum(jnp.abs(gen32 - real), axis=1, keepdims=True) * (0.5 / C) + 1e-05
        dmd = ((fake - real) / spread).astype(bf16).astype(f32)
        cot[...] = dmd + adversarial

    @pl.when(role != 1)
    def _():
        lane = lanes((ROWS, 128))
        full = cot[...]
        c_high = full.astype(bf16).astype(f32)
        cot2 = jnp.where(lane < C, c_high, full - c_high).astype(bf16)
        for c in range(CHUNKS):
            cs = pl.ds(c * CHUNK, CHUNK)
            hcot = (dot_nt(cot2, r2_all[slot, cs, :]) * slope[:, cs]).astype(bf16)
            x_ref[:, cs] = dot(z_t[...], hcot)
        x_ref[C : C + 1, :] = x_ref[C : C + 1, :] + x_ref[C + 1 : C + 2, :]
        stage_a_fill(t_a, False)
        h_a = stage_a(t_a, e_a, send_h, recv_h)
        start(h_a)
        arrive(h_a)
        summed = total(t_a[p], e_a)
        t_b[...] = summed.astype(bf16)
        h_b = stage_b(t_b, e_b, send_h, recv_h)
        start(h_b)
        arrive(h_b)
        summed = total(summed, e_b)
        h_buf[pl.ds(own_top, 16), pl.ds(own_left, HALF)] = summed[:, :HALF].astype(bf16)
        h_c = stage_c(h_buf, send_h, recv_h)
        start(h_c)
        put_row(summed[:, HALF:])
        left = lt[...] * (1.0 / math.sqrt(ROWS * SIDE * SIDE))
        l_high, l_low = split(left[:, :C])
        base = left[:, C : C + 1] * vrow[0:1, :]
        arrive(h_c)
        full_h = h_buf[...]
        grads[0] = base + dot(l_high, full_h) + dot(l_low, full_h)
        finish(h_a)
        finish(h_b)
        finish(h_c)


def shards(sn, sc, lv, emb, tim, gain, blk, rdo):
    vmem = pl.BlockSpec(memory_space=pltpu.VMEM)
    scratch = [
        ((C, ROWS), bf16), ((C, ROWS), bf16), ((ROWS // 128, 128), f32), ((1, C, D), bf16),
        ((1, D), f32), ((1, D), f32), ((1, DEPTH, F), bf16), ((1, C, F), bf16),
        ((80, F), f32), ((16, 128), f32), ((8, F), f32),
        ((SIDE, 16, HALF + 256), bf16), ((SIDE, 16, HALF + 256), bf16),
        ((16, HALF + 256), bf16), ((SIDE, 16, HALF + 256), bf16),
        ((2, 128, F), bf16), ((8, F), f32), ((ROWS, 128), f32),
        ((C, F), bf16), ((8, ROWS), f32), ((8, ROWS), f32),
        ((SIDE, 16, HALF + 128), bf16), ((SIDE, 16, HALF + 128), bf16),
        ((16, HALF + 128), bf16), ((SIDE, 16, HALF + 128), bf16), ((C, F), bf16),
        ((2, F, 128), bf16), ((3, 128, 128), bf16), ((ROWS, 128), f32), ((ROWS, 128), f32),
        ((2, ROWS, 128), bf16), ((80, ROWS), bf16), ((2, ROWS, CHUNK), f32), ((ROWS, 128), f32),
        ((ROWS, F), f32), ((ROWS, F), f32),
        ((DEPTH, 128), f32), ((ROWS, 128), f32),
        ((ROWS, 128), f32),
        ((ROWS // 2, 128), bf16), ((ROWS // 2, 128), bf16), ((ROWS // 2, 128), bf16),
        ((4, ROWS // 2, 128), bf16),
    ]
    dma = pltpu.SemaphoreType.DMA
    grads, generated = pl.pallas_call(
        kernel,
        out_shape=(
            jax.ShapeDtypeStruct((1, DEPTH, F), f32),
            jax.ShapeDtypeStruct((C, ROWS), bf16),
        ),
        in_specs=[pl.BlockSpec(memory_space=pltpu.HBM)] * 8,
        out_specs=(vmem, vmem),
        scratch_shapes=[pltpu.VMEM(shape, kind) for shape, kind in scratch]
        + [dma((8,))]
        + [dma((3, SIDE)) for _ in range(4)]
        + [dma((1,)), dma((1,)), dma((1,)), dma((4,)), dma((11,)), dma((11,))]
        + [pltpu.SemaphoreType.REGULAR],
        compiler_params=pltpu.CompilerParams(
            collective_id=0, has_side_effects=True, vmem_limit_bytes=32 * 2**20
        ),
    )(
        *(
            pltpu.with_memory_space_constraint(array, pltpu.HBM)
            for array in (
                sn.T, sc.T, lv.reshape(ROWS // 128, 128), emb, tim, gain, blk,
                rdo.transpose(0, 2, 1),
            )
        )
    )
    return grads, generated.T


def solution(mesh):
    in_specs = (
        P("fsdp", None),
        P("fsdp", None),
        P("fsdp"),
        P("role", None, None),
        P("role", None),
        P("role", None),
        P("role", "fsdp", None),
        P("role", None, None),
    )
    out_specs = (P("role", "fsdp", None), P("fsdp", None))
    return jax.shard_map(shards, mesh=mesh, in_specs=in_specs, out_specs=out_specs, check_vma=False)
```

```python
import functools
import math

import jax
import jax.numpy as jnp
from jax import lax
from jax.experimental import pallas as pl
from jax.experimental.pallas import tpu as pltpu
from jax.sharding import PartitionSpec as P

MESH = pl.DeviceIdType.MESH
f32, bf16 = jnp.float32, jnp.bfloat16
adv_weight = 3.0
ROWS = 384
C = 64
D = 3072
F = 1536
DEPTH = 48
CHUNK = 256
CHUNKS = F // CHUNK
SIDE = 8
HALF = F // 2
YX_ORDER = (5, 3, 4, 7, 1, 6, 2)
Z_ORDER = (4, 5, 3, 6, 2, 7, 1)
ROOT = math.sqrt(2.0 / math.pi)
CUBE = 0.044715 * ROOT


def dot(a, b):
    return jnp.dot(a, b, preferred_element_type=f32)


def dot_nt(a, b):
    return lax.dot_general(a, b, (((1,), (1,)), ((), ())), preferred_element_type=f32)


def split(value):
    high = value.astype(bf16)
    return high, (value - high.astype(f32)).astype(bf16)


def lanes(shape):
    return lax.broadcasted_iota(jnp.int32, shape, len(shape) - 1)


def pack(value):
    top, bottom = value[: ROWS // 2], value[ROWS // 2 :]
    return jnp.where(lanes(top.shape) < C, top, bottom)


def unpack(value):
    turned = pltpu.roll(value, C, 1)
    left = lanes(value.shape) < C
    return jnp.concatenate([jnp.where(left, value, turned), jnp.where(left, turned, value)], axis=0)


def gelu_parts(hidden):
    square = hidden * hidden
    half = 0.5 + 0.5 * jnp.tanh(hidden * (ROOT + CUBE * square))
    return square, half, hidden * half


def gelu_slope(square, half, value):
    return half + value * (1.0 - half) * (2.0 * ROOT + 6.0 * CUBE * square)


def kernel(
    *refs,
):
    hbm, (grads, gen_out), scratch, (fetch, *sems) = refs[:8], refs[8:10], refs[10:-12], refs[-12:]
    step(hbm, fetch, grads, gen_out, *scratch, *sems)


def step(
    hbm, fetch, grads, gen_out,
    sn, sc, lv, emb, tim, gain, blk, rdo, x_ref, vt, vrow, s_a, d_a, s_b, d_b, m_all, rsum, gen_f, rd_in, rs_row, rs_in,
    t_a, e_a, t_b, e_b, e_c, h_buf,
    r2_all, gram, level, z_f32, z_all, z_t, rs_all, y_ref, hid, slope, lt, cot,
    noise_in, gen_pk, gen_in, out_pk, col_in,
    send_m, recv_m, send_h, recv_h, send_g, recv_g, send_c, recv_c, send_x, recv_x, turn,
):
    role = lax.axis_index("role")
    place = lax.axis_index("fsdp")
    p, z = place // SIDE, place % SIDE
    slot = jnp.where(role == 0, 0, 1)

    def yx_peer(k):
        return (role, lax.rem(p + k, SIDE) * SIDE + z)

    def z_peer(k):
        return (role, p * SIDE + lax.rem(z + k, SIDE))

    def role_peer(k):
        return (lax.rem(role + k, 4), place)

    barrier = pltpu.get_barrier_semaphore()
    for k_yx, k_z in zip(YX_ORDER, Z_ORDER):
        pl.semaphore_signal(barrier, inc=1, device_id=yx_peer(k_yx), device_id_type=MESH)
        pl.semaphore_signal(barrier, inc=1, device_id=z_peer(k_z), device_id_type=MESH)
    for k in range(1, 4):
        pl.semaphore_signal(barrier, inc=1, device_id=role_peer(k), device_id_type=MESH)

    fetches = [
        pltpu.make_async_copy(src, dst, fetch.at[i])
        for i, (src, dst) in enumerate(zip(hbm, (sn, sc, lv, emb, tim, gain, blk, rdo)))
    ]
    for i in (4, 5, 3, 6, 7, 0, 1, 2):
        fetches[i].start()

    def remote(src, dst, send, recv, device):
        return pltpu.make_async_remote_copy(
            src_ref=src, dst_ref=dst, send_sem=send, recv_sem=recv, device_id=device,
            device_id_type=MESH,
        )

    begin = place * DEPTH
    window = jnp.minimum(begin // 128, D // 128 - 2) * 128
    window = pl.multiple_of(window, 128)
    wide = pl.ds(window, 256)
    for i in (4, 5, 3, 6):
        fetches[i].wait()
    gain_w = gain[:, wide]
    lifted = jnp.concatenate(
        [
            emb[0, :, wide].astype(f32) * gain_w,
            jnp.where(
                lax.broadcasted_iota(jnp.int32, (16, 256), 0) == 0, tim[:, wide] * gain_w, 0.0
            ),
        ],
        axis=0,
    )
    lifted = pltpu.roll(lifted, lax.rem(256 + window - begin, 256), 1)[:, :128]
    high, low = split(lifted[:, :DEPTH])
    block = blk[0]
    x_ref[...] = dot(high, block) + dot(low, block)

    def stage_a_fill(send, low_too):
        vt[...] = jnp.zeros_like(vt)
        for i in range(F // 128):
            vt[i : i + 1, :] = x_ref[C : C + 1, i * 128 : i * 128 + 128]
        tile = vt[...]
        for piece in range(SIDE):
            top, left = piece // 2 * 16, piece % 2 * HALF
            send[piece, :, :HALF] = x_ref[top : top + 16, left : left + HALF].astype(bf16)
            v_high, v_low = split(tile)
            send[piece, :, HALF : HALF + 128] = v_high
            if low_too:
                send[piece, :, HALF + 128 :] = v_low

    def stage_a(send, dest, ss, rr):
        return [
            remote(send.at[lax.rem(p + k, SIDE)], dest.at[k], ss.at[0, k], rr.at[0, k], yx_peer(k))
            for k in YX_ORDER
        ]

    def stage_b(send, dest, ss, rr):
        return [
            remote(send, dest.at[k], ss.at[1, k], rr.at[1, k], z_peer(k)) for k in Z_ORDER
        ]

    own_top = pl.multiple_of(p // 2 * 16, 16)
    own_left = pl.multiple_of(lax.rem(p, 2) * HALF, 128)

    other_left = pl.multiple_of(HALF - own_left, 128)
    own_block = (pl.ds(own_top, 16), pl.ds(own_left, HALF))

    def stage_c(buf, ss, rr):
        own = buf.at[own_block]
        return [remote(own, own, ss.at[2, k], rr.at[2, k], yx_peer(k)) for k in YX_ORDER]

    def start(copies):
        for copy in copies:
            copy.start()

    def arrive(copies):
        for copy in copies:
            copy.wait_recv()

    def finish(copies):
        for copy in copies:
            copy.wait_send()

    def total(first, dest):
        value = first.astype(f32)
        for k in range(1, SIDE):
            value = value + dest[k].astype(f32)
        return value

    def put_row(tile):
        vt[...] = tile
        for i in range(F // 128):
            vrow[0:1, i * 128 : i * 128 + 128] = vt[i : i + 1, :]

    stage_a_fill(s_a, True)
    pl.semaphore_wait(barrier, 2 * (SIDE - 1) + 3)
    m_a = stage_a(s_a, d_a, send_m, recv_m)

    @pl.when(role == 1)
    def _():
        pl.semaphore_wait(turn, 1)

    start(m_a)

    for i in (0, 1, 2, 7):
        fetches[i].wait()

    lt[...] = jnp.concatenate([lifted, jnp.zeros((48, 128), f32)], axis=0).T[:DEPTH]
    for i in range(ROWS // 128):
        level[i * 128 : i * 128 + 128, :] = jnp.broadcast_to(lv[i : i + 1, :], (128, 128)).T
    readout = rdo[0].astype(f32)
    rsum[...] = dot(jnp.ones((16, C), bf16), rdo[0])[:8]
    r2_all[slot] = jnp.concatenate([readout, readout], axis=0).T.astype(bf16)
    time = tim[...]
    t_1 = time.astype(bf16).astype(f32)
    t_2 = (time - t_1).astype(bf16).astype(f32)
    t_3 = time - t_1 - t_2
    rows = lax.broadcasted_iota(jnp.int32, (16, D), 0)
    parts = jnp.where(rows == 0, t_1, jnp.where(rows == 1, t_2, jnp.where(rows == 2, t_3, 0.0)))
    square_e = dot_nt(emb[0], emb[0])
    cross = jnp.sum(dot_nt(parts.astype(bf16), emb[0]), axis=0, keepdims=True)
    square_e = jnp.concatenate([square_e, square_e], axis=1)
    cross = jnp.concatenate([cross, cross], axis=1)
    square_t = jnp.sum(time * time, axis=1, keepdims=True)
    g_1, rest = split(square_e)
    rest = square_e - g_1.astype(f32)
    g_2, g_3 = split(rest)
    for i, part in enumerate((g_1, g_2, g_3)):
        gram[i, :C] = part
        gram[i, C:] = jnp.zeros((C, 128), bf16)
    m_all[0, 80:, :] = jnp.zeros((48, F), bf16)
    m_all[1, 80:, :] = jnp.zeros((48, F), bf16)

    def rows_with(latent, lev):
        lane = lanes((ROWS, 128))
        lev_high = lev.astype(bf16).astype(f32)
        return jnp.where(
            lane < C,
            latent,
            jnp.where(lane < C + 2, lev_high, jnp.where(lane == C + 2, lev - lev_high, 0.0)),
        ).astype(bf16)

    def rows_in(to, latent, lev):
        z_f32[...] = latent
        z16 = rows_with(latent, lev)
        z_all[to] = z16
        y = dot(z16, gram[0]) + dot(z16, gram[1]) + dot(z16, gram[2]) + lev * cross
        y_ref[...] = y
        mean = (
            0.5 * jnp.sum(latent * (y + lev * cross), axis=1, keepdims=True)
            + lev[:, :1] * lev[:, :1] * square_t
        ) * (1.0 / D)
        rs_all[to] = jnp.broadcast_to(lax.rsqrt(jnp.maximum(mean, 0.0) + 1e-06), (ROWS, CHUNK))

    def rows_turned():
        lane = lanes((ROWS, 128))
        lev = jnp.where(role == 0, 1.0, level[...])
        lev_high = lev.astype(bf16).astype(f32)
        turned = jnp.where(
            lane < C,
            z_f32[...],
            jnp.where(lane == C, lev_high, jnp.where(lane == C + 1, lev - lev_high, 0.0)),
        ).T
        z_t[...] = turned[:80].astype(bf16)

    critic_here = (3, place)
    x_readout = remote(rdo.at[0], rd_in, send_x.at[8], recv_x.at[8], critic_here)
    x_scales = remote(rs_row, rs_in, send_x.at[9], recv_x.at[9], critic_here)
    level_rows = m_all.at[0, pl.ds(C, 16), :]
    x_level = remote(level_rows, level_rows, send_x.at[10], recv_x.at[10], critic_here)
    matrix_block = m_all.at[(0, *own_block)]
    x_matrix = {
        k: remote(
            matrix_block, matrix_block, send_x.at[k], recv_x.at[k],
            (3, lax.rem(p + k, SIDE) * SIDE + z),
        )
        for k in (*YX_ORDER, 0)
    }

    arrive(m_a)

    @pl.when(role == 0)
    def _():
        pl.semaphore_signal(
            turn, inc=1, device_id=(jnp.where(role == 0, 1, 2), place), device_id_type=MESH
        )

    summed = total(s_a[p], d_a)
    s_b[:, :HALF] = summed[:, :HALF].astype(bf16)
    v_high, v_low = split(summed[:, HALF : HALF + 128] + summed[:, HALF + 128 :])
    s_b[:, HALF : HALF + 128] = v_high
    s_b[:, HALF + 128 :] = v_low
    m_b = stage_b(s_b, d_b, send_m, recv_m)
    start(m_b)

    @pl.when((role == 0) | (role == 3))
    def _():
        noise = sn[...].astype(f32)
        noise = jnp.concatenate([noise, noise], axis=0).T

        @pl.when(role == 0)
        def _():
            x_readout.start()
            rows_in(0, noise, jnp.ones((ROWS, 128), f32))
            rs_row[...] = rs_all[0, :, :128].T[:8]
            x_scales.start()

        @pl.when(role == 3)
        def _():
            z_all[0] = rows_with(noise, jnp.ones((ROWS, 128), f32))

    @pl.when(role != 0)
    def _():
        noise = sc[...].astype(f32)
        noise_in[...] = level[...] * jnp.concatenate([noise, noise], axis=0).T

    arrive(m_b)
    summed = total(summed, d_b)
    m_all[(slot, *own_block)] = summed[:, :HALF].astype(bf16)
    m_c = dict(zip(YX_ORDER, stage_c(m_all.at[slot], send_m, recv_m)))

    @pl.when(role == 0)
    def _():
        for k in YX_ORDER:
            x_matrix[k].start()

    start(m_c.values())
    put_row(summed[:, HALF : HALF + 128] + summed[:, HALF + 128 :])
    v_full = vrow[0:1, :]
    v_high = v_full.astype(bf16).astype(f32)
    rows = lax.broadcasted_iota(jnp.int32, (16, F), 0)
    m_all[slot, C : C + 16, :] = jnp.where(
        (rows == 0) | (rows == 2), v_high, jnp.where(rows == 1, v_full - v_high, 0.0)
    ).astype(bf16)

    @pl.when(role == 0)
    def _():
        x_level.start()
        x_matrix[0].start()

    near, far = (2, 4, 6), (1, 3, 5, 7)

    @pl.when(role != 0)
    def _():
        arrive(m_c.values())

    @pl.when(role == 3)
    def _():
        x_readout.wait_recv()
        first = rd_in[...].astype(f32)
        r2_all[0] = jnp.concatenate([first, first], axis=0).T.astype(bf16)
        x_scales.wait_recv()
        for i in range(ROWS // 128):
            here = slice(i * 128, i * 128 + 128)
            scales = jnp.broadcast_to(rs_in[0:1, here], (128, 128)).T
            rs_all[0, here, :128] = scales
            rs_all[0, here, 128:] = scales
        x_level.wait_recv()

    def columns(c):
        left = own_left if c < CHUNKS // 2 else other_left
        return pl.ds(pl.multiple_of(left + c % (CHUNKS // 2) * CHUNK, CHUNK), CHUNK)

    def forward(net, critic, before=None, slopes_too=False):
        out = jnp.zeros((ROWS, 128), f32)
        through = jnp.zeros((ROWS, 128), f32)
        for c in range(CHUNKS):
            if before and c % (CHUNKS // 2) == 0:
                before(c)
            cs = columns(c)
            hidden = dot(z_all[net], m_all[net, :, cs]) * rs_all[net]
            square, half, value = gelu_parts(hidden)
            out += dot(value.astype(bf16), r2_all[net, cs, :])
            if critic or slopes_too:
                rise = gelu_slope(square, half, value)
                slope[:, cs] = rise * rs_all[net]
            if critic:
                through += dot_nt((rise * rsum[0:1, cs]).astype(bf16), m_all[net, :, cs])
            if not (critic or slopes_too):
                hid[:, cs] = hidden
        return out.astype(bf16).astype(f32), through

    def slopes():
        for c in range(CHUNKS):
            cs = pl.ds(c * CHUNK, CHUNK)
            slope[:, cs] = gelu_slope(*gelu_parts(hid[:, cs])) * rs_all[slot]

    hand_on = remote(
        gen_pk, gen_in, send_g.at[0], recv_g.at[0], (jnp.where(role == 0, 1, 2), place)
    )

    def to_gen(source, device):
        return remote(
            out_pk, col_in.at[source], send_c.at[0], recv_c.at[source], (device, place)
        )

    @pl.when((role == 0) | (role == 3))
    def _():
        def matrix_in(c):
            @pl.when(role == 0)
            def _():
                arrive([m_c[k] for k in (near if c == 0 else far)])

            @pl.when(role == 3)
            def _():
                arrive([x_matrix[k] for k in ((0, *near) if c == 0 else far)])

        out, unused = forward(0, False, matrix_in)
        gen_f[...] = out
        gen_pk[...] = pack(out).astype(bf16)
        hand_on.start()

    @pl.when(role == 0)
    def _():
        slopes()
        rows_turned()
        finish(x_matrix.values())
        finish((x_readout, x_scales, x_level, hand_on))

    @pl.when(role != 0)
    def _():
        @pl.when(role != 3)
        def _():
            hand_on.wait_recv()
            gen_f[...] = unpack(gen_in[...].astype(f32))

        lev = level[...]
        noised = (1.0 - lev) * gen_f[...] + noise_in[...]
        rows_in(1, noised.astype(bf16).astype(f32), lev)

        @pl.when(role == 3)
        def _():
            out, through = forward(1, True)
            logit = 0.5 * jnp.sum(out, axis=1, keepdims=True)
            down = -1.0 / (1.0 + jnp.exp(logit))
            pulled = jnp.sum(z_all[1].astype(f32) * through, axis=1, keepdims=True)
            latent = jnp.where(lanes((ROWS, 128)) < C, through, pltpu.roll(through, C, 1))
            inverse = rs_all[1, :, :128]
            back = inverse * (latent - inverse * inverse * (1.0 / D) * pulled * y_ref[...])
            out_pk[...] = pack(adv_weight * (1.0 - lev) * down * back).astype(bf16)
            to_gen(3, 0).start()
            cot[...] = jnp.broadcast_to(1.0 / (1.0 + jnp.exp(-logit)), (ROWS, 128))
            hand_on.wait_send()

        @pl.when(role != 3)
        def _():
            out, unused = forward(1, False, None, True)
            out_pk[...] = pack(out).astype(bf16)
            to_gen(role, 0).start()
            cot[...] = out - gen_f[...]

        @pl.when(role != 1)
        def _():
            rows_turned()

        to_gen(role, 0).wait_send()

    finish(m_a)
    finish(m_b)
    finish(m_c.values())

    @pl.when(role == 1)
    def _():
        gen_out[...] = gen_f[...].T[:C].astype(bf16)
        grads[...] = jnp.zeros_like(grads)

    @pl.when(role == 0)
    def _():
        for source in (1, 2, 3):
            to_gen(source, source).wait_recv()
        real, fake, adversarial = [unpack(col_in[k].astype(f32)) for k in (1, 2, 3)]
        gen32 = gen_f[...]
        spread = jnp.sum(jnp.abs(gen32 - real), axis=1, keepdims=True) * (0.5 / C) + 1e-05
        dmd = ((fake - real) / spread).astype(bf16).astype(f32)
        cot[...] = dmd + adversarial

    @pl.when(role != 1)
    def _():
        lane = lanes((ROWS, 128))
        full = cot[...]
        c_high = full.astype(bf16).astype(f32)
        cot2 = jnp.where(lane < C, c_high, full - c_high).astype(bf16)
        h_a = {copy_k: copy for copy_k, copy in zip(YX_ORDER, stage_a(t_a, e_a, send_h, recv_h))}

        def row_tile(value):
            value_high = value.astype(bf16).astype(f32)
            return jnp.concatenate([value_high, value - value_high], axis=0).astype(bf16)

        def half_out(left, offsets):
            for c in range(CHUNKS // 2):
                cs = pl.ds(pl.multiple_of(left + c * CHUNK, CHUNK), CHUNK)
                hcot = (dot_nt(cot2, r2_all[slot, cs, :]) * slope[:, cs]).astype(bf16)
                x_ref[:, cs] = dot(z_t[...], hcot)
            for i in range(HALF // 128):
                here = pl.ds(pl.multiple_of(left + i * 128, 128), 128)
                vt[i : i + 1, :] = x_ref[C : C + 1, here] + x_ref[C + 1 : C + 2, here]
            tile = row_tile(vt[0:8, :])
            for k in offsets:
                piece = lax.rem(p + k, SIDE)
                top = pl.multiple_of(piece // 2 * 16, 16)
                t_a[piece, :, :HALF] = x_ref[pl.ds(top, 16), pl.ds(left, HALF)].astype(bf16)
                t_a[piece, :, HALF:] = tile
                if k:
                    h_a[k].start()

        vt[...] = jnp.zeros_like(vt)
        half_out(other_left, (5, 3, 7, 1))
        half_out(own_left, (4, 2, 6, 0))
        gen_out[...] = gen_f[...].T[:C].astype(bf16)
        left = lt[...] * (1.0 / math.sqrt(ROWS * SIDE * SIDE))
        l_high, l_low = split(left[:, :C])
        arrive(h_a.values())
        summed = total(t_a[p], e_a)
        t_b[:, :HALF] = summed[:, :HALF].astype(bf16)
        t_b[:, HALF:] = row_tile(summed[0:8, HALF:] + summed[8:16, HALF:])
        h_b = stage_b(t_b, e_b, send_h, recv_h)
        start(h_b)
        arrive(h_b)
        summed = total(summed, e_b)
        e_c[0, :, :HALF] = summed[:, :HALF].astype(bf16)
        e_c[0, :, HALF:] = row_tile(summed[0:8, HALF:] + summed[8:16, HALF:])
        h_c = {
            k: remote(e_c.at[0], e_c.at[k], send_h.at[2, k], recv_h.at[2, k], yx_peer(k))
            for k in YX_ORDER
        }
        start(h_c.values())
        for k in (0, 6, 2, 4, 1, 7, 3, 5):
            if k:
                h_c[k].wait_recv()
            piece = lax.rem(p + SIDE - k, SIDE)
            block = pl.ds(pl.multiple_of(lax.rem(piece, 2) * HALF, 128), HALF)
            h_buf[pl.ds(pl.multiple_of(piece // 2 * 16, 16), 16), block] = e_c[k, :, :HALF]
            if k < 2:
                tile = e_c[k, :, HALF:].astype(f32)
                vt[0:8, :] = tile[0:8] + tile[8:16]
                for i in range(HALF // 128):
                    here = pl.ds(
                        pl.multiple_of((own_left if k == 0 else other_left) + i * 128, 128), 128
                    )
                    vrow[0:1, here] = vt[i : i + 1, :]
        full_h = h_buf[...]
        grads[0] = left[:, C : C + 1] * vrow[0:1, :] + dot(l_high, full_h) + dot(l_low, full_h)
        finish(h_a.values())
        finish(h_b)
        finish(h_c.values())


def shards(sn, sc, lv, emb, tim, gain, blk, rdo):
    vmem = pl.BlockSpec(memory_space=pltpu.VMEM)
    scratch = [
        ((C, ROWS), bf16), ((C, ROWS), bf16), ((ROWS // 128, 128), f32), ((1, C, D), bf16),
        ((1, D), f32), ((1, D), f32), ((1, DEPTH, F), bf16), ((1, C, F), bf16),
        ((80, F), f32), ((16, 128), f32), ((8, F), f32),
        ((SIDE, 16, HALF + 256), bf16), ((SIDE, 16, HALF + 256), bf16),
        ((16, HALF + 256), bf16), ((SIDE, 16, HALF + 256), bf16),
        ((2, 128, F), bf16), ((8, F), f32), ((ROWS, 128), f32),
        ((C, F), bf16), ((8, ROWS), f32), ((8, ROWS), f32),
        ((SIDE, 16, HALF + 128), bf16), ((SIDE, 16, HALF + 128), bf16),
        ((16, HALF + 128), bf16), ((SIDE, 16, HALF + 128), bf16),
        ((SIDE, 16, HALF + 128), bf16), ((C, F), bf16),
        ((2, F, 128), bf16), ((3, 128, 128), bf16), ((ROWS, 128), f32), ((ROWS, 128), f32),
        ((2, ROWS, 128), bf16), ((80, ROWS), bf16), ((2, ROWS, CHUNK), f32), ((ROWS, 128), f32),
        ((ROWS, F), f32), ((ROWS, F), f32),
        ((DEPTH, 128), f32), ((ROWS, 128), f32),
        ((ROWS, 128), f32),
        ((ROWS // 2, 128), bf16), ((ROWS // 2, 128), bf16), ((ROWS // 2, 128), bf16),
        ((4, ROWS // 2, 128), bf16),
    ]
    dma = pltpu.SemaphoreType.DMA
    grads, generated = pl.pallas_call(
        kernel,
        out_shape=(
            jax.ShapeDtypeStruct((1, DEPTH, F), f32),
            jax.ShapeDtypeStruct((C, ROWS), bf16),
        ),
        in_specs=[pl.BlockSpec(memory_space=pltpu.HBM)] * 8,
        out_specs=(vmem, vmem),
        scratch_shapes=[pltpu.VMEM(shape, kind) for shape, kind in scratch]
        + [dma((8,))]
        + [dma((3, SIDE)) for _ in range(4)]
        + [dma((1,)), dma((1,)), dma((1,)), dma((4,)), dma((11,)), dma((11,))]
        + [pltpu.SemaphoreType.REGULAR],
        compiler_params=pltpu.CompilerParams(
            collective_id=0, has_side_effects=True, vmem_limit_bytes=32 * 2**20
        ),
    )(
        *(
            pltpu.with_memory_space_constraint(array, pltpu.HBM)
            for array in (
                sn.T, sc.T, lv.reshape(ROWS // 128, 128), emb, tim, gain, blk,
                rdo.transpose(0, 2, 1),
            )
        )
    )
    return grads, generated.T


def solution(mesh):
    in_specs = (
        P("fsdp", None),
        P("fsdp", None),
        P("fsdp"),
        P("role", None, None),
        P("role", None),
        P("role", None),
        P("role", "fsdp", None),
        P("role", None, None),
    )
    out_specs = (P("role", "fsdp", None), P("fsdp", None))
    return jax.shard_map(shards, mesh=mesh, in_specs=in_specs, out_specs=out_specs, check_vma=False)
```

```python
import functools
import math

import jax
import jax.numpy as jnp
from jax import lax
from jax.experimental import pallas as pl
from jax.experimental.pallas import tpu as pltpu
from jax.sharding import PartitionSpec as P

MESH = pl.DeviceIdType.MESH
f32, bf16 = jnp.float32, jnp.bfloat16
adv_weight = 3.0
ROWS = 384
C = 64
D = 3072
F = 1536
DEPTH = 48
CHUNK = 256
CHUNKS = F // CHUNK
SIDE = 8
HALF = F // 2
YX_ORDER = (5, 3, 4, 7, 1, 6, 2)
Z_ORDER = (4, 5, 3, 6, 2, 7, 1)
ROOT = math.sqrt(2.0 / math.pi)
CUBE = 0.044715 * ROOT


def dot(a, b):
    return jnp.dot(a, b, preferred_element_type=f32)


def dot_nt(a, b):
    return lax.dot_general(a, b, (((1,), (1,)), ((), ())), preferred_element_type=f32)


def split(value):
    high = value.astype(bf16)
    return high, (value - high.astype(f32)).astype(bf16)


def lanes(shape):
    return lax.broadcasted_iota(jnp.int32, shape, len(shape) - 1)


def pack(value):
    top, bottom = value[: ROWS // 2], value[ROWS // 2 :]
    return jnp.where(lanes(top.shape) < C, top, bottom)


def unpack(value):
    turned = pltpu.roll(value, C, 1)
    left = lanes(value.shape) < C
    return jnp.concatenate([jnp.where(left, value, turned), jnp.where(left, turned, value)], axis=0)


def row_tile(value):
    value_high = value.astype(bf16).astype(f32)
    return jnp.concatenate([value_high, value - value_high], axis=0).astype(bf16)


def gelu_parts(hidden):
    square = hidden * hidden
    half = 0.5 + 0.5 * jnp.tanh(hidden * (ROOT + CUBE * square))
    return square, half, hidden * half


def gelu_slope(square, half, value):
    return half + value * (1.0 - half) * (2.0 * ROOT + 6.0 * CUBE * square)


def kernel(
    *refs,
):
    hbm, (grads, gen_out), scratch, (fetch, *sems) = refs[:8], refs[8:10], refs[10:-12], refs[-12:]
    step(hbm, fetch, grads, gen_out, *scratch, *sems)


def step(
    hbm, fetch, grads, gen_out,
    sn, sc, lv, emb, tim, gain, blk, rdo, x_ref, vt, vrow, s_a, d_a, s_b, d_b, m_all, tiles, rsum, gen_f, rd_in, rs_row, rs_in,
    t_a, e_a, t_b, e_b, e_c, h_buf,
    r2_all, gram, level, z_f32, z_all, z_t, rs_all, y_ref, hid, slope, lt, cot,
    noise_in, gen_pk, gen_in, out_pk, col_in,
    send_m, recv_m, send_h, recv_h, send_g, recv_g, send_c, recv_c, send_x, recv_x, turn,
):
    role = lax.axis_index("role")
    place = lax.axis_index("fsdp")
    p, z = place // SIDE, place % SIDE
    slot = jnp.where(role == 0, 0, 1)

    def yx_peer(k):
        return (role, lax.rem(p + k, SIDE) * SIDE + z)

    def z_peer(k):
        return (role, p * SIDE + lax.rem(z + k, SIDE))

    def role_peer(k):
        return (lax.rem(role + k, 4), place)

    barrier = pltpu.get_barrier_semaphore()
    for k_yx, k_z in zip(YX_ORDER, Z_ORDER):
        pl.semaphore_signal(barrier, inc=1, device_id=yx_peer(k_yx), device_id_type=MESH)
        pl.semaphore_signal(barrier, inc=1, device_id=z_peer(k_z), device_id_type=MESH)
    for k in range(1, 4):
        pl.semaphore_signal(barrier, inc=1, device_id=role_peer(k), device_id_type=MESH)

    fetches = [
        pltpu.make_async_copy(src, dst, fetch.at[i])
        for i, (src, dst) in enumerate(zip(hbm, (sn, sc, lv, emb, tim, gain, blk, rdo)))
    ]
    for i in (4, 5, 3, 6, 7, 0, 1, 2):
        fetches[i].start()

    def remote(src, dst, send, recv, device):
        return pltpu.make_async_remote_copy(
            src_ref=src, dst_ref=dst, send_sem=send, recv_sem=recv, device_id=device,
            device_id_type=MESH,
        )

    begin = place * DEPTH
    window = jnp.minimum(begin // 128, D // 128 - 2) * 128
    window = pl.multiple_of(window, 128)
    wide = pl.ds(window, 256)
    for i in (4, 5, 3, 6):
        fetches[i].wait()
    gain_w = gain[:, wide]
    lifted = jnp.concatenate(
        [
            emb[0, :, wide].astype(f32) * gain_w,
            jnp.where(
                lax.broadcasted_iota(jnp.int32, (16, 256), 0) == 0, tim[:, wide] * gain_w, 0.0
            ),
        ],
        axis=0,
    )
    lifted = pltpu.roll(lifted, lax.rem(256 + window - begin, 256), 1)[:, :128]
    high, low = split(lifted[:, :DEPTH])
    block = blk[0]
    x_ref[...] = dot(high, block) + dot(low, block)

    def stage_a_fill(send):
        vt[...] = jnp.zeros_like(vt)
        for side in range(2):
            for i in range(HALF // 128):
                here = slice(side * HALF + i * 128, side * HALF + i * 128 + 128)
                vt[i : i + 1, :] = x_ref[C : C + 1, here]
            tile = row_tile(vt[0:8, :])
            for piece in range(side, SIDE, 2):
                top = piece // 2 * 16
                part = x_ref[top : top + 16, side * HALF : side * HALF + HALF]
                send[piece, :, :HALF] = part.astype(bf16)
                send[piece, :, HALF:] = tile

    def stage_a(send, dest, ss, rr):
        return [
            remote(send.at[lax.rem(p + k, SIDE)], dest.at[k], ss.at[0, k], rr.at[0, k], yx_peer(k))
            for k in YX_ORDER
        ]

    def stage_b(send, dest, ss, rr):
        return [
            remote(send, dest.at[k], ss.at[1, k], rr.at[1, k], z_peer(k)) for k in Z_ORDER
        ]

    own_top = pl.multiple_of(p // 2 * 16, 16)
    own_left = pl.multiple_of(lax.rem(p, 2) * HALF, 128)

    other_left = pl.multiple_of(HALF - own_left, 128)
    own_block = (pl.ds(own_top, 16), pl.ds(own_left, HALF))

    def stage_c(buf, ss, rr):
        own = buf.at[own_block]
        return [remote(own, own, ss.at[2, k], rr.at[2, k], yx_peer(k)) for k in YX_ORDER]

    def start(copies):
        for copy in copies:
            copy.start()

    def arrive(copies):
        for copy in copies:
            copy.wait_recv()

    def finish(copies):
        for copy in copies:
            copy.wait_send()

    def total(first, dest):
        values = [first.astype(f32)] + [dest[k].astype(f32) for k in range(1, SIDE)]
        while len(values) > 1:
            values = [a + b for a, b in zip(values[::2], values[1::2])]
        return values[0]

    stage_a_fill(s_a)
    pl.semaphore_wait(barrier, 2 * (SIDE - 1) + 3)
    m_a = stage_a(s_a, d_a, send_m, recv_m)

    @pl.when(role == 1)
    def _():
        pl.semaphore_wait(turn, 1)

    start(m_a)

    for i in (0, 1, 2, 7):
        fetches[i].wait()

    lt[...] = jnp.concatenate([lifted, jnp.zeros((48, 128), f32)], axis=0).T[:DEPTH]
    for i in range(ROWS // 128):
        level[i * 128 : i * 128 + 128, :] = jnp.broadcast_to(lv[i : i + 1, :], (128, 128)).T
    readout = rdo[0].astype(f32)
    rsum[...] = dot(jnp.ones((16, C), bf16), rdo[0])[:8]
    r2_all[slot] = jnp.concatenate([readout, readout], axis=0).T.astype(bf16)
    time = tim[...]
    t_1 = time.astype(bf16).astype(f32)
    t_2 = (time - t_1).astype(bf16).astype(f32)
    t_3 = time - t_1 - t_2
    rows = lax.broadcasted_iota(jnp.int32, (16, D), 0)
    parts = jnp.where(rows == 0, t_1, jnp.where(rows == 1, t_2, jnp.where(rows == 2, t_3, 0.0)))
    square_e = dot_nt(emb[0], emb[0])
    cross = jnp.sum(dot_nt(parts.astype(bf16), emb[0]), axis=0, keepdims=True)
    square_e = jnp.concatenate([square_e, square_e], axis=1)
    cross = jnp.concatenate([cross, cross], axis=1)
    square_t = jnp.sum(time * time, axis=1, keepdims=True)
    g_1, rest = split(square_e)
    rest = square_e - g_1.astype(f32)
    g_2, g_3 = split(rest)
    for i, part in enumerate((g_1, g_2, g_3)):
        gram[i, :C] = part
        gram[i, C:] = jnp.zeros((C, 128), bf16)
    m_all[0, 80:, :] = jnp.zeros((48, F), bf16)
    m_all[1, 80:, :] = jnp.zeros((48, F), bf16)

    def rows_with(latent, lev):
        lane = lanes((ROWS, 128))
        lev_high = lev.astype(bf16).astype(f32)
        return jnp.where(
            lane < C,
            latent,
            jnp.where(lane < C + 2, lev_high, jnp.where(lane == C + 2, lev - lev_high, 0.0)),
        ).astype(bf16)

    def rows_in(to, latent, lev):
        z_f32[...] = latent
        z16 = rows_with(latent, lev)
        z_all[to] = z16
        y = dot(z16, gram[0]) + dot(z16, gram[1]) + dot(z16, gram[2]) + lev * cross
        y_ref[...] = y
        mean = (
            0.5 * jnp.sum(latent * (y + lev * cross), axis=1, keepdims=True)
            + lev[:, :1] * lev[:, :1] * square_t
        ) * (1.0 / D)
        rs_all[to] = jnp.broadcast_to(lax.rsqrt(jnp.maximum(mean, 0.0) + 1e-06), (ROWS, CHUNK))

    def rows_turned():
        lane = lanes((ROWS, 128))
        lev = jnp.where(role == 0, 1.0, level[...])
        lev_high = lev.astype(bf16).astype(f32)
        turned = jnp.where(
            lane < C,
            z_f32[...],
            jnp.where(lane == C, lev_high, jnp.where(lane == C + 1, lev - lev_high, 0.0)),
        ).T
        z_t[...] = turned[:80].astype(bf16)

    critic_here = (3, place)
    x_readout = remote(rdo.at[0], rd_in, send_x.at[8], recv_x.at[8], critic_here)
    x_scales = remote(rs_row, rs_in, send_x.at[9], recv_x.at[9], critic_here)
    beside = lax.rem(p + 1, SIDE) * SIDE + z
    x_own = remote(tiles.at[0], tiles.at[2], send_x.at[10], recv_x.at[10], critic_here)
    x_other = remote(tiles.at[0], tiles.at[3], send_x.at[11], recv_x.at[11], (3, beside))
    x_tile = remote(tiles.at[0], tiles.at[1], send_x.at[12], recv_x.at[12], (role, beside))
    matrix_block = m_all.at[(0, *own_block)]
    x_matrix = {
        k: remote(
            matrix_block, matrix_block, send_x.at[k], recv_x.at[k],
            (3, lax.rem(p + k, SIDE) * SIDE + z),
        )
        for k in (*YX_ORDER, 0)
    }

    arrive(m_a)

    @pl.when(role == 0)
    def _():
        pl.semaphore_signal(
            turn, inc=1, device_id=(jnp.where(role == 0, 1, 2), place), device_id_type=MESH
        )

    summed = total(s_a[p], d_a)
    s_b[:, :HALF] = summed[:, :HALF].astype(bf16)
    s_b[:, HALF:] = row_tile(summed[0:8, HALF:] + summed[8:16, HALF:])
    m_b = stage_b(s_b, d_b, send_m, recv_m)
    start(m_b)

    @pl.when((role == 0) | (role == 3))
    def _():
        noise = sn[...].astype(f32)
        noise = jnp.concatenate([noise, noise], axis=0).T

        @pl.when(role == 0)
        def _():
            x_readout.start()
            rows_in(0, noise, jnp.ones((ROWS, 128), f32))
            rs_row[...] = rs_all[0, :, :128].T[:8]
            x_scales.start()

        @pl.when(role == 3)
        def _():
            z_all[0] = rows_with(noise, jnp.ones((ROWS, 128), f32))

    @pl.when(role != 0)
    def _():
        noise = sc[...].astype(f32)
        noise_in[...] = level[...] * jnp.concatenate([noise, noise], axis=0).T

    arrive(m_b)
    summed = total(summed, d_b)
    m_all[(slot, *own_block)] = summed[:, :HALF].astype(bf16)
    m_c = dict(zip(YX_ORDER, stage_c(m_all.at[slot], send_m, recv_m)))

    @pl.when(role == 0)
    def _():
        for k in YX_ORDER:
            x_matrix[k].start()

    start(m_c.values())
    tiles[0] = row_tile(summed[0:8, HALF:] + summed[8:16, HALF:])
    x_tile.start()

    @pl.when(role == 0)
    def _():
        x_own.start()
        x_other.start()
        x_matrix[0].start()

    def level_rows(net, left, tile):
        rows = lax.broadcasted_iota(jnp.int32, (16, 128), 0)
        value = tile.astype(f32)
        for i in range(HALF // 128):
            here = pl.ds(pl.multiple_of(left + i * 128, 128), 128)
            m_all[net, C : C + 16, here] = jnp.where(
                (rows == 0) | (rows == 2),
                value[i : i + 1],
                jnp.where(rows == 1, value[8 + i : 9 + i], 0.0),
            ).astype(bf16)

    level_rows(slot, own_left, tiles[0])
    x_tile.wait_recv()
    level_rows(slot, other_left, tiles[1])

    near, far = (2, 4, 6), (1, 3, 5, 7)

    @pl.when(role != 0)
    def _():
        arrive(m_c.values())

    @pl.when(role == 3)
    def _():
        x_readout.wait_recv()
        first = rd_in[...].astype(f32)
        r2_all[0] = jnp.concatenate([first, first], axis=0).T.astype(bf16)
        x_scales.wait_recv()
        for i in range(ROWS // 128):
            here = slice(i * 128, i * 128 + 128)
            scales = jnp.broadcast_to(rs_in[0:1, here], (128, 128)).T
            rs_all[0, here, :128] = scales
            rs_all[0, here, 128:] = scales
        x_own.wait_recv()
        level_rows(0, own_left, tiles[2])
        x_other.wait_recv()
        level_rows(0, other_left, tiles[3])

    def columns(c):
        left = own_left if c < CHUNKS // 2 else other_left
        return pl.ds(pl.multiple_of(left + c % (CHUNKS // 2) * CHUNK, CHUNK), CHUNK)

    def forward(net, critic, before=None, slopes_too=False):
        out = jnp.zeros((ROWS, 128), f32)
        through = jnp.zeros((ROWS, 128), f32)
        for c in range(CHUNKS):
            if before and c % (CHUNKS // 2) == 0:
                before(c)
            cs = columns(c)
            hidden = dot(z_all[net], m_all[net, :, cs]) * rs_all[net]
            square, half, value = gelu_parts(hidden)
            out += dot(value.astype(bf16), r2_all[net, cs, :])
            if critic or slopes_too:
                rise = gelu_slope(square, half, value)
                slope[:, cs] = rise * rs_all[net]
            if critic:
                through += dot_nt((rise * rsum[0:1, cs]).astype(bf16), m_all[net, :, cs])
            if not (critic or slopes_too):
                hid[:, cs] = hidden
        return out.astype(bf16).astype(f32), through

    def slopes():
        for c in range(CHUNKS):
            cs = pl.ds(c * CHUNK, CHUNK)
            slope[:, cs] = gelu_slope(*gelu_parts(hid[:, cs])) * rs_all[slot]

    hand_on = remote(
        gen_pk, gen_in, send_g.at[0], recv_g.at[0], (jnp.where(role == 0, 1, 2), place)
    )

    def to_gen(source, device):
        return remote(
            out_pk, col_in.at[source], send_c.at[0], recv_c.at[source], (device, place)
        )

    @pl.when((role == 0) | (role == 3))
    def _():
        def matrix_in(c):
            @pl.when(role == 0)
            def _():
                arrive([m_c[k] for k in (near if c == 0 else far)])

            @pl.when(role == 3)
            def _():
                arrive([x_matrix[k] for k in ((0, *near) if c == 0 else far)])

        out, unused = forward(0, False, matrix_in)
        gen_f[...] = out
        gen_pk[...] = pack(out).astype(bf16)
        hand_on.start()

    @pl.when(role == 0)
    def _():
        slopes()
        rows_turned()
        finish(x_matrix.values())
        finish((x_readout, x_scales, x_own, x_other, hand_on))

    @pl.when(role != 0)
    def _():
        @pl.when(role != 3)
        def _():
            hand_on.wait_recv()
            gen_f[...] = unpack(gen_in[...].astype(f32))

        lev = level[...]
        noised = (1.0 - lev) * gen_f[...] + noise_in[...]
        rows_in(1, noised.astype(bf16).astype(f32), lev)

        @pl.when(role == 3)
        def _():
            out, through = forward(1, True)
            logit = 0.5 * jnp.sum(out, axis=1, keepdims=True)
            down = -1.0 / (1.0 + jnp.exp(logit))
            pulled = jnp.sum(z_all[1].astype(f32) * through, axis=1, keepdims=True)
            latent = jnp.where(lanes((ROWS, 128)) < C, through, pltpu.roll(through, C, 1))
            inverse = rs_all[1, :, :128]
            back = inverse * (latent - inverse * inverse * (1.0 / D) * pulled * y_ref[...])
            out_pk[...] = pack(adv_weight * (1.0 - lev) * down * back).astype(bf16)
            to_gen(3, 0).start()
            cot[...] = jnp.broadcast_to(1.0 / (1.0 + jnp.exp(-logit)), (ROWS, 128))
            hand_on.wait_send()

        @pl.when(role != 3)
        def _():
            out, unused = forward(1, False, None, True)
            out_pk[...] = pack(out).astype(bf16)
            to_gen(role, 0).start()
            cot[...] = out - gen_f[...]

        @pl.when(role != 1)
        def _():
            rows_turned()

        to_gen(role, 0).wait_send()

    finish(m_a)
    finish(m_b)
    finish(m_c.values())
    x_tile.wait_send()

    @pl.when(role == 1)
    def _():
        gen_out[...] = gen_f[...].T[:C].astype(bf16)
        grads[...] = jnp.zeros_like(grads)

    @pl.when(role == 0)
    def _():
        for source in (1, 2, 3):
            to_gen(source, source).wait_recv()
        real, fake, adversarial = [unpack(col_in[k].astype(f32)) for k in (1, 2, 3)]
        gen32 = gen_f[...]
        spread = jnp.sum(jnp.abs(gen32 - real), axis=1, keepdims=True) * (0.5 / C) + 1e-05
        dmd = ((fake - real) / spread).astype(bf16).astype(f32)
        cot[...] = dmd + adversarial

    @pl.when(role != 1)
    def _():
        lane = lanes((ROWS, 128))
        full = cot[...]
        c_high = full.astype(bf16).astype(f32)
        cot2 = jnp.where(lane < C, c_high, full - c_high).astype(bf16)
        h_a = {copy_k: copy for copy_k, copy in zip(YX_ORDER, stage_a(t_a, e_a, send_h, recv_h))}

        def half_out(left, offsets):
            for c in range(CHUNKS // 2):
                cs = pl.ds(pl.multiple_of(left + c * CHUNK, CHUNK), CHUNK)
                hcot = (dot_nt(cot2, r2_all[slot, cs, :]) * slope[:, cs]).astype(bf16)
                x_ref[:, cs] = dot(z_t[...], hcot)
            for i in range(HALF // 128):
                here = pl.ds(pl.multiple_of(left + i * 128, 128), 128)
                vt[i : i + 1, :] = x_ref[C : C + 1, here] + x_ref[C + 1 : C + 2, here]
            tile = row_tile(vt[0:8, :])
            for k in offsets:
                piece = lax.rem(p + k, SIDE)
                top = pl.multiple_of(piece // 2 * 16, 16)
                t_a[piece, :, :HALF] = x_ref[pl.ds(top, 16), pl.ds(left, HALF)].astype(bf16)
                t_a[piece, :, HALF:] = tile
                if k:
                    h_a[k].start()

        vt[...] = jnp.zeros_like(vt)
        half_out(other_left, (5, 3, 7, 1))
        half_out(own_left, (4, 2, 6, 0))
        gen_out[...] = gen_f[...].T[:C].astype(bf16)
        left = lt[...] * (1.0 / math.sqrt(ROWS * SIDE * SIDE))
        l_high, l_low = split(left[:, :C])
        arrive(h_a.values())
        summed = total(t_a[p], e_a)
        t_b[:, :HALF] = summed[:, :HALF].astype(bf16)
        t_b[:, HALF:] = row_tile(summed[0:8, HALF:] + summed[8:16, HALF:])
        h_b = stage_b(t_b, e_b, send_h, recv_h)
        start(h_b)
        arrive(h_b)
        summed = total(summed, e_b)
        e_c[0, :, :HALF] = summed[:, :HALF].astype(bf16)
        e_c[0, :, HALF:] = row_tile(summed[0:8, HALF:] + summed[8:16, HALF:])
        h_c = {
            k: remote(e_c.at[0], e_c.at[k], send_h.at[2, k], recv_h.at[2, k], yx_peer(k))
            for k in YX_ORDER
        }
        start(h_c.values())
        for k in (0, 6, 2, 4, 1, 7, 3, 5):
            if k:
                h_c[k].wait_recv()
            piece = lax.rem(p + SIDE - k, SIDE)
            block = pl.ds(pl.multiple_of(lax.rem(piece, 2) * HALF, 128), HALF)
            h_buf[pl.ds(pl.multiple_of(piece // 2 * 16, 16), 16), block] = e_c[k, :, :HALF]
            if k < 2:
                tile = e_c[k, :, HALF:].astype(f32)
                vt[0:8, :] = tile[0:8] + tile[8:16]
                for i in range(HALF // 128):
                    here = pl.ds(
                        pl.multiple_of((own_left if k == 0 else other_left) + i * 128, 128), 128
                    )
                    vrow[0:1, here] = vt[i : i + 1, :]
        full_h = h_buf[...]
        grads[0] = left[:, C : C + 1] * vrow[0:1, :] + dot(l_high, full_h) + dot(l_low, full_h)
        finish(h_a.values())
        finish(h_b)
        finish(h_c.values())


def shards(sn, sc, lv, emb, tim, gain, blk, rdo):
    vmem = pl.BlockSpec(memory_space=pltpu.VMEM)
    scratch = [
        ((C, ROWS), bf16), ((C, ROWS), bf16), ((ROWS // 128, 128), f32), ((1, C, D), bf16),
        ((1, D), f32), ((1, D), f32), ((1, DEPTH, F), bf16), ((1, C, F), bf16),
        ((80, F), f32), ((16, 128), f32), ((8, F), f32),
        ((SIDE, 16, HALF + 128), bf16), ((SIDE, 16, HALF + 128), bf16),
        ((16, HALF + 128), bf16), ((SIDE, 16, HALF + 128), bf16),
        ((2, 128, F), bf16), ((4, 16, 128), bf16), ((8, F), f32), ((ROWS, 128), f32),
        ((C, F), bf16), ((8, ROWS), f32), ((8, ROWS), f32),
        ((SIDE, 16, HALF + 128), bf16), ((SIDE, 16, HALF + 128), bf16),
        ((16, HALF + 128), bf16), ((SIDE, 16, HALF + 128), bf16),
        ((SIDE, 16, HALF + 128), bf16), ((C, F), bf16),
        ((2, F, 128), bf16), ((3, 128, 128), bf16), ((ROWS, 128), f32), ((ROWS, 128), f32),
        ((2, ROWS, 128), bf16), ((80, ROWS), bf16), ((2, ROWS, CHUNK), f32), ((ROWS, 128), f32),
        ((ROWS, F), f32), ((ROWS, F), f32),
        ((DEPTH, 128), f32), ((ROWS, 128), f32),
        ((ROWS, 128), f32),
        ((ROWS // 2, 128), bf16), ((ROWS // 2, 128), bf16), ((ROWS // 2, 128), bf16),
        ((4, ROWS // 2, 128), bf16),
    ]
    dma = pltpu.SemaphoreType.DMA
    grads, generated = pl.pallas_call(
        kernel,
        out_shape=(
            jax.ShapeDtypeStruct((1, DEPTH, F), f32),
            jax.ShapeDtypeStruct((C, ROWS), bf16),
        ),
        in_specs=[pl.BlockSpec(memory_space=pltpu.HBM)] * 8,
        out_specs=(vmem, vmem),
        scratch_shapes=[pltpu.VMEM(shape, kind) for shape, kind in scratch]
        + [dma((8,))]
        + [dma((3, SIDE)) for _ in range(4)]
        + [dma((1,)), dma((1,)), dma((1,)), dma((4,)), dma((13,)), dma((13,))]
        + [pltpu.SemaphoreType.REGULAR],
        compiler_params=pltpu.CompilerParams(
            collective_id=0, has_side_effects=True, vmem_limit_bytes=32 * 2**20
        ),
    )(
        *(
            pltpu.with_memory_space_constraint(array, pltpu.HBM)
            for array in (
                sn.T, sc.T, lv.reshape(ROWS // 128, 128), emb, tim, gain, blk,
                rdo.transpose(0, 2, 1),
            )
        )
    )
    return grads, generated.T


def solution(mesh):
    in_specs = (
        P("fsdp", None),
        P("fsdp", None),
        P("fsdp"),
        P("role", None, None),
        P("role", None),
        P("role", None),
        P("role", "fsdp", None),
        P("role", None, None),
    )
    out_specs = (P("role", "fsdp", None), P("fsdp", None))
    return jax.shard_map(shards, mesh=mesh, in_specs=in_specs, out_specs=out_specs, check_vma=False)
```

```python
import functools
import math

import jax
import jax.numpy as jnp
from jax import lax
from jax.experimental import pallas as pl
from jax.experimental.pallas import tpu as pltpu
from jax.sharding import PartitionSpec as P

MESH = pl.DeviceIdType.MESH
f32, bf16 = jnp.float32, jnp.bfloat16
adv_weight = 3.0
ROWS = 384
C = 64
D = 3072
F = 1536
DEPTH = 48
CHUNK = 768
CHUNKS = F // CHUNK
SIDE = 8
HALF = F // 2
YX_ORDER = (5, 3, 4, 7, 1, 6, 2)
Z_ORDER = (4, 5, 3, 6, 2, 7, 1)
ROOT = math.sqrt(2.0 / math.pi)
CUBE = 0.044715 * ROOT


def dot(a, b):
    return jnp.dot(a, b, preferred_element_type=f32)


def dot_nt(a, b):
    return lax.dot_general(a, b, (((1,), (1,)), ((), ())), preferred_element_type=f32)


def split(value):
    high = value.astype(bf16)
    return high, (value - high.astype(f32)).astype(bf16)


def lanes(shape):
    return lax.broadcasted_iota(jnp.int32, shape, len(shape) - 1)


def pack(value):
    top, bottom = value[: ROWS // 2], value[ROWS // 2 :]
    return jnp.where(lanes(top.shape) < C, top, bottom)


def unpack(value):
    turned = pltpu.roll(value, C, 1)
    left = lanes(value.shape) < C
    return jnp.concatenate([jnp.where(left, value, turned), jnp.where(left, turned, value)], axis=0)


def row_tile(value):
    value_high = value.astype(bf16).astype(f32)
    return jnp.concatenate([value_high, value - value_high], axis=0).astype(bf16)


def gelu_parts(hidden):
    square = hidden * hidden
    half = 0.5 + 0.5 * jnp.tanh(hidden * (ROOT + CUBE * square))
    return square, half, hidden * half


def gelu_slope(square, half, value):
    return half + value * (1.0 - half) * (2.0 * ROOT + 6.0 * CUBE * square)


def kernel(
    *refs,
):
    hbm, (grads, gen_out), scratch, (fetch, *sems) = refs[:8], refs[8:10], refs[10:-12], refs[-12:]
    step(hbm, fetch, grads, gen_out, *scratch, *sems)


def step(
    hbm, fetch, grads, gen_out,
    sn, sc, lv, emb, tim, gain, blk, rdo, x_ref, vt, vrow, s_a, d_a, s_b, d_b, m_all, tiles, rsum, gen_f, rd_in, rs_row, rs_in,
    t_a, e_a, t_b, e_b, e_c, h_buf,
    r2_all, gram, level, z_f32, z_all, z_t, rs_all, y_ref, hid, slope, lt, cot,
    noise_in, gen_pk, gen_in, out_pk, col_in,
    send_m, recv_m, send_h, recv_h, send_g, recv_g, send_c, recv_c, send_x, recv_x, turn,
):
    role = lax.axis_index("role")
    place = lax.axis_index("fsdp")
    p, z = place // SIDE, place % SIDE
    slot = jnp.where(role == 0, 0, 1)

    def yx_peer(k):
        return (role, lax.rem(p + k, SIDE) * SIDE + z)

    def z_peer(k):
        return (role, p * SIDE + lax.rem(z + k, SIDE))

    def role_peer(k):
        return (lax.rem(role + k, 4), place)

    barrier = pltpu.get_barrier_semaphore()
    for k_yx, k_z in zip(YX_ORDER, Z_ORDER):
        pl.semaphore_signal(barrier, inc=1, device_id=yx_peer(k_yx), device_id_type=MESH)
        pl.semaphore_signal(barrier, inc=1, device_id=z_peer(k_z), device_id_type=MESH)
    for k in range(1, 4):
        pl.semaphore_signal(barrier, inc=1, device_id=role_peer(k), device_id_type=MESH)

    fetches = [
        pltpu.make_async_copy(src, dst, fetch.at[i])
        for i, (src, dst) in enumerate(zip(hbm, (sn, sc, lv, emb, tim, gain, blk, rdo)))
    ]
    for i in (4, 5, 3, 6, 7, 0, 1, 2):
        fetches[i].start()

    def remote(src, dst, send, recv, device):
        return pltpu.make_async_remote_copy(
            src_ref=src, dst_ref=dst, send_sem=send, recv_sem=recv, device_id=device,
            device_id_type=MESH,
        )

    begin = place * DEPTH
    window = jnp.minimum(begin // 128, D // 128 - 2) * 128
    window = pl.multiple_of(window, 128)
    wide = pl.ds(window, 256)
    for i in (4, 5, 3, 6):
        fetches[i].wait()
    gain_w = gain[:, wide]
    lifted = jnp.concatenate(
        [
            emb[0, :, wide].astype(f32) * gain_w,
            jnp.where(
                lax.broadcasted_iota(jnp.int32, (16, 256), 0) == 0, tim[:, wide] * gain_w, 0.0
            ),
        ],
        axis=0,
    )
    lifted = pltpu.roll(lifted, lax.rem(256 + window - begin, 256), 1)[:, :128]
    high, low = split(lifted[:, :DEPTH])
    block = blk[0]
    x_ref[...] = dot(high, block) + dot(low, block)

    def stage_a_fill(send):
        vt[...] = jnp.zeros_like(vt)
        for side in range(2):
            for i in range(HALF // 128):
                here = slice(side * HALF + i * 128, side * HALF + i * 128 + 128)
                vt[i : i + 1, :] = x_ref[C : C + 1, here]
            tile = row_tile(vt[0:8, :])
            for piece in range(side, SIDE, 2):
                top = piece // 2 * 16
                part = x_ref[top : top + 16, side * HALF : side * HALF + HALF]
                send[piece, :, :HALF] = part.astype(bf16)
                send[piece, :, HALF:] = tile

    def stage_a(send, dest, ss, rr):
        return [
            remote(send.at[lax.rem(p + k, SIDE)], dest.at[k], ss.at[0, k], rr.at[0, k], yx_peer(k))
            for k in YX_ORDER
        ]

    def stage_b(send, dest, ss, rr):
        return [
            remote(send, dest.at[k], ss.at[1, k], rr.at[1, k], z_peer(k)) for k in Z_ORDER
        ]

    own_top = pl.multiple_of(p // 2 * 16, 16)
    own_left = pl.multiple_of(lax.rem(p, 2) * HALF, 128)

    other_left = pl.multiple_of(HALF - own_left, 128)
    own_block = (pl.ds(own_top, 16), pl.ds(own_left, HALF))

    def stage_c(buf, ss, rr):
        own = buf.at[own_block]
        return [remote(own, own, ss.at[2, k], rr.at[2, k], yx_peer(k)) for k in YX_ORDER]

    def start(copies):
        for copy in copies:
            copy.start()

    def arrive(copies):
        for copy in copies:
            copy.wait_recv()

    def finish(copies):
        for copy in copies:
            copy.wait_send()

    def total(first, dest):
        values = [first.astype(f32)] + [dest[k].astype(f32) for k in range(1, SIDE)]
        while len(values) > 1:
            values = [a + b for a, b in zip(values[::2], values[1::2])]
        return values[0]

    stage_a_fill(s_a)
    pl.semaphore_wait(barrier, 2 * (SIDE - 1) + 3)
    m_a = stage_a(s_a, d_a, send_m, recv_m)

    @pl.when(role == 1)
    def _():
        pl.semaphore_wait(turn, 1)

    start(m_a)

    for i in (0, 1, 2, 7):
        fetches[i].wait()

    lt[...] = jnp.concatenate([lifted, jnp.zeros((48, 128), f32)], axis=0).T[:DEPTH]
    for i in range(ROWS // 128):
        level[i * 128 : i * 128 + 128, :] = jnp.broadcast_to(lv[i : i + 1, :], (128, 128)).T
    readout = rdo[0].astype(f32)
    rsum[...] = dot(jnp.ones((16, C), bf16), rdo[0])[:8]
    r2_all[slot] = jnp.concatenate([readout, readout], axis=0).T.astype(bf16)
    time = tim[...]
    t_1 = time.astype(bf16).astype(f32)
    t_2 = (time - t_1).astype(bf16).astype(f32)
    t_3 = time - t_1 - t_2
    rows = lax.broadcasted_iota(jnp.int32, (16, D), 0)
    parts = jnp.where(rows == 0, t_1, jnp.where(rows == 1, t_2, jnp.where(rows == 2, t_3, 0.0)))
    square_e = dot_nt(emb[0], emb[0])
    cross = jnp.sum(dot_nt(parts.astype(bf16), emb[0]), axis=0, keepdims=True)
    square_e = jnp.concatenate([square_e, square_e], axis=1)
    cross = jnp.concatenate([cross, cross], axis=1)
    square_t = jnp.sum(time * time, axis=1, keepdims=True)
    g_1, rest = split(square_e)
    rest = square_e - g_1.astype(f32)
    g_2, g_3 = split(rest)
    for i, part in enumerate((g_1, g_2, g_3)):
        gram[i, :C] = part
        gram[i, C:] = jnp.zeros((C, 128), bf16)
    m_all[0, 80:, :] = jnp.zeros((48, F), bf16)
    m_all[1, 80:, :] = jnp.zeros((48, F), bf16)

    def rows_with(latent, lev):
        lane = lanes((ROWS, 128))
        lev_high = lev.astype(bf16).astype(f32)
        return jnp.where(
            lane < C,
            latent,
            jnp.where(lane < C + 2, lev_high, jnp.where(lane == C + 2, lev - lev_high, 0.0)),
        ).astype(bf16)

    def rows_in(to, latent, lev):
        z_f32[...] = latent
        z16 = rows_with(latent, lev)
        z_all[to] = z16
        y = dot(z16, gram[0]) + dot(z16, gram[1]) + dot(z16, gram[2]) + lev * cross
        y_ref[...] = y
        mean = (
            0.5 * jnp.sum(latent * (y + lev * cross), axis=1, keepdims=True)
            + lev[:, :1] * lev[:, :1] * square_t
        ) * (1.0 / D)
        rs_all[to] = jnp.broadcast_to(lax.rsqrt(jnp.maximum(mean, 0.0) + 1e-06), (ROWS, CHUNK))

    def rows_turned():
        lane = lanes((ROWS, 128))
        lev = jnp.where(role == 0, 1.0, level[...])
        lev_high = lev.astype(bf16).astype(f32)
        turned = jnp.where(
            lane < C,
            z_f32[...],
            jnp.where(lane == C, lev_high, jnp.where(lane == C + 1, lev - lev_high, 0.0)),
        ).T
        z_t[...] = turned[:80].astype(bf16)

    critic_here = (3, place)
    x_readout = remote(rdo.at[0], rd_in, send_x.at[8], recv_x.at[8], critic_here)
    x_scales = remote(rs_row, rs_in, send_x.at[9], recv_x.at[9], critic_here)
    beside = lax.rem(p + 1, SIDE) * SIDE + z
    x_own = remote(tiles.at[0], tiles.at[2], send_x.at[10], recv_x.at[10], critic_here)
    x_other = remote(tiles.at[0], tiles.at[3], send_x.at[11], recv_x.at[11], (3, beside))
    x_tile = remote(tiles.at[0], tiles.at[1], send_x.at[12], recv_x.at[12], (role, beside))
    matrix_block = m_all.at[(0, *own_block)]
    x_matrix = {
        k: remote(
            matrix_block, matrix_block, send_x.at[k], recv_x.at[k],
            (3, lax.rem(p + k, SIDE) * SIDE + z),
        )
        for k in (*YX_ORDER, 0)
    }

    arrive(m_a)

    @pl.when(role == 0)
    def _():
        pl.semaphore_signal(
            turn, inc=1, device_id=(jnp.where(role == 0, 1, 2), place), device_id_type=MESH
        )

    summed = total(s_a[p], d_a)
    s_b[:, :HALF] = summed[:, :HALF].astype(bf16)
    s_b[:, HALF:] = row_tile(summed[0:8, HALF:] + summed[8:16, HALF:])
    m_b = stage_b(s_b, d_b, send_m, recv_m)
    start(m_b)

    @pl.when((role == 0) | (role == 3))
    def _():
        noise = sn[...].astype(f32)
        noise = jnp.concatenate([noise, noise], axis=0).T

        @pl.when(role == 0)
        def _():
            x_readout.start()
            rows_in(0, noise, jnp.ones((ROWS, 128), f32))
            rs_row[...] = rs_all[0, :, :128].T[:8]
            x_scales.start()

        @pl.when(role == 3)
        def _():
            z_all[0] = rows_with(noise, jnp.ones((ROWS, 128), f32))

    @pl.when(role != 0)
    def _():
        noise = sc[...].astype(f32)
        noise_in[...] = level[...] * jnp.concatenate([noise, noise], axis=0).T

    arrive(m_b)
    summed = total(summed, d_b)
    m_all[(slot, *own_block)] = summed[:, :HALF].astype(bf16)
    m_c = dict(zip(YX_ORDER, stage_c(m_all.at[slot], send_m, recv_m)))

    @pl.when(role == 0)
    def _():
        for k in YX_ORDER:
            x_matrix[k].start()

    start(m_c.values())
    tiles[0] = row_tile(summed[0:8, HALF:] + summed[8:16, HALF:])
    x_tile.start()

    @pl.when(role == 0)
    def _():
        x_own.start()
        x_other.start()
        x_matrix[0].start()

    def level_rows(net, left, tile):
        rows = lax.broadcasted_iota(jnp.int32, (16, 128), 0)
        value = tile.astype(f32)
        for i in range(HALF // 128):
            here = pl.ds(pl.multiple_of(left + i * 128, 128), 128)
            m_all[net, C : C + 16, here] = jnp.where(
                (rows == 0) | (rows == 2),
                value[i : i + 1],
                jnp.where(rows == 1, value[8 + i : 9 + i], 0.0),
            ).astype(bf16)

    level_rows(slot, own_left, tiles[0])
    x_tile.wait_recv()
    level_rows(slot, other_left, tiles[1])

    near, far = (2, 4, 6), (1, 3, 5, 7)

    @pl.when(role != 0)
    def _():
        arrive(m_c.values())

    @pl.when(role == 3)
    def _():
        x_readout.wait_recv()
        first = rd_in[...].astype(f32)
        r2_all[0] = jnp.concatenate([first, first], axis=0).T.astype(bf16)
        x_scales.wait_recv()
        for i in range(ROWS // 128):
            here = slice(i * 128, i * 128 + 128)
            scales = jnp.broadcast_to(rs_in[0:1, here], (128, 128)).T
            rs_all[0, here, :] = jnp.concatenate([scales] * (CHUNK // 128), axis=1)
        x_own.wait_recv()
        level_rows(0, own_left, tiles[2])
        x_other.wait_recv()
        level_rows(0, other_left, tiles[3])

    def columns(c):
        left = own_left if c < CHUNKS // 2 else other_left
        return pl.ds(pl.multiple_of(left + c % (CHUNKS // 2) * CHUNK, CHUNK), CHUNK)

    def forward(net, critic, before=None, slopes_too=False):
        out = jnp.zeros((ROWS, 128), f32)
        through = jnp.zeros((ROWS, 128), f32)
        for c in range(CHUNKS):
            if before and c % (CHUNKS // 2) == 0:
                before(c)
            cs = columns(c)
            hidden = dot(z_all[net], m_all[net, :, cs]) * rs_all[net]
            square, half, value = gelu_parts(hidden)
            out += dot(value.astype(bf16), r2_all[net, cs, :])
            if critic or slopes_too:
                rise = gelu_slope(square, half, value)
                slope[:, cs] = rise * rs_all[net]
            if critic:
                through += dot_nt((rise * rsum[0:1, cs]).astype(bf16), m_all[net, :, cs])
            if not (critic or slopes_too):
                hid[:, cs] = hidden
        return out.astype(bf16).astype(f32), through

    def slopes():
        for c in range(CHUNKS):
            cs = pl.ds(c * CHUNK, CHUNK)
            slope[:, cs] = gelu_slope(*gelu_parts(hid[:, cs])) * rs_all[slot]

    hand_on = remote(
        gen_pk, gen_in, send_g.at[0], recv_g.at[0], (jnp.where(role == 0, 1, 2), place)
    )

    def to_gen(source, device):
        return remote(
            out_pk, col_in.at[source], send_c.at[0], recv_c.at[source], (device, place)
        )

    @pl.when((role == 0) | (role == 3))
    def _():
        def matrix_in(c):
            @pl.when(role == 0)
            def _():
                arrive([m_c[k] for k in (near if c == 0 else far)])

            @pl.when(role == 3)
            def _():
                arrive([x_matrix[k] for k in ((0, *near) if c == 0 else far)])

        out, unused = forward(0, False, matrix_in)
        gen_f[...] = out
        gen_pk[...] = pack(out).astype(bf16)
        hand_on.start()

    @pl.when(role == 0)
    def _():
        slopes()
        rows_turned()
        finish(x_matrix.values())
        finish((x_readout, x_scales, x_own, x_other, hand_on))

    @pl.when(role != 0)
    def _():
        @pl.when(role != 3)
        def _():
            hand_on.wait_recv()
            gen_f[...] = unpack(gen_in[...].astype(f32))

        lev = level[...]
        noised = (1.0 - lev) * gen_f[...] + noise_in[...]
        rows_in(1, noised.astype(bf16).astype(f32), lev)

        @pl.when(role == 3)
        def _():
            out, through = forward(1, True)
            logit = 0.5 * jnp.sum(out, axis=1, keepdims=True)
            down = -1.0 / (1.0 + jnp.exp(logit))
            pulled = jnp.sum(z_all[1].astype(f32) * through, axis=1, keepdims=True)
            latent = jnp.where(lanes((ROWS, 128)) < C, through, pltpu.roll(through, C, 1))
            inverse = rs_all[1, :, :128]
            back = inverse * (latent - inverse * inverse * (1.0 / D) * pulled * y_ref[...])
            out_pk[...] = pack(adv_weight * (1.0 - lev) * down * back).astype(bf16)
            to_gen(3, 0).start()
            cot[...] = jnp.broadcast_to(1.0 / (1.0 + jnp.exp(-logit)), (ROWS, 128))
            hand_on.wait_send()

        @pl.when(role != 3)
        def _():
            out, unused = forward(1, False, None, True)
            out_pk[...] = pack(out).astype(bf16)
            to_gen(role, 0).start()
            cot[...] = out - gen_f[...]

        @pl.when(role != 1)
        def _():
            rows_turned()

        to_gen(role, 0).wait_send()

    finish(m_a)
    finish(m_b)
    finish(m_c.values())
    x_tile.wait_send()

    @pl.when(role == 1)
    def _():
        gen_out[...] = gen_f[...].T[:C].astype(bf16)
        grads[...] = jnp.zeros_like(grads)

    @pl.when(role == 0)
    def _():
        for source in (1, 2, 3):
            to_gen(source, source).wait_recv()
        real, fake, adversarial = [unpack(col_in[k].astype(f32)) for k in (1, 2, 3)]
        gen32 = gen_f[...]
        spread = jnp.sum(jnp.abs(gen32 - real), axis=1, keepdims=True) * (0.5 / C) + 1e-05
        dmd = ((fake - real) / spread).astype(bf16).astype(f32)
        cot[...] = dmd + adversarial

    @pl.when(role != 1)
    def _():
        lane = lanes((ROWS, 128))
        full = cot[...]
        c_high = full.astype(bf16).astype(f32)
        cot2 = jnp.where(lane < C, c_high, full - c_high).astype(bf16)
        h_a = {copy_k: copy for copy_k, copy in zip(YX_ORDER, stage_a(t_a, e_a, send_h, recv_h))}

        def half_out(left, offsets):
            for c in range(CHUNKS // 2):
                cs = pl.ds(pl.multiple_of(left + c * CHUNK, CHUNK), CHUNK)
                hcot = (dot_nt(cot2, r2_all[slot, cs, :]) * slope[:, cs]).astype(bf16)
                x_ref[:, cs] = dot(z_t[...], hcot)
            for i in range(HALF // 128):
                here = pl.ds(pl.multiple_of(left + i * 128, 128), 128)
                vt[i : i + 1, :] = x_ref[C : C + 1, here] + x_ref[C + 1 : C + 2, here]
            tile = row_tile(vt[0:8, :])
            for k in offsets:
                piece = lax.rem(p + k, SIDE)
                top = pl.multiple_of(piece // 2 * 16, 16)
                t_a[piece, :, :HALF] = x_ref[pl.ds(top, 16), pl.ds(left, HALF)].astype(bf16)
                t_a[piece, :, HALF:] = tile
                if k:
                    h_a[k].start()

        vt[...] = jnp.zeros_like(vt)
        half_out(other_left, (5, 3, 7, 1))
        half_out(own_left, (4, 2, 6, 0))
        gen_out[...] = gen_f[...].T[:C].astype(bf16)
        left = lt[...] * (1.0 / math.sqrt(ROWS * SIDE * SIDE))
        l_high, l_low = split(left[:, :C])
        arrive(h_a.values())
        summed = total(t_a[p], e_a)
        t_b[:, :HALF] = summed[:, :HALF].astype(bf16)
        t_b[:, HALF:] = row_tile(summed[0:8, HALF:] + summed[8:16, HALF:])
        h_b = stage_b(t_b, e_b, send_h, recv_h)
        start(h_b)
        arrive(h_b)
        summed = total(summed, e_b)
        e_c[0, :, :HALF] = summed[:, :HALF].astype(bf16)
        e_c[0, :, HALF:] = row_tile(summed[0:8, HALF:] + summed[8:16, HALF:])
        h_c = {
            k: remote(e_c.at[0], e_c.at[k], send_h.at[2, k], recv_h.at[2, k], yx_peer(k))
            for k in YX_ORDER
        }
        start(h_c.values())
        for k in (0, 6, 2, 4, 1, 7, 3, 5):
            if k:
                h_c[k].wait_recv()
            piece = lax.rem(p + SIDE - k, SIDE)
            block = pl.ds(pl.multiple_of(lax.rem(piece, 2) * HALF, 128), HALF)
            h_buf[pl.ds(pl.multiple_of(piece // 2 * 16, 16), 16), block] = e_c[k, :, :HALF]
            if k < 2:
                tile = e_c[k, :, HALF:].astype(f32)
                vt[0:8, :] = tile[0:8] + tile[8:16]
                for i in range(HALF // 128):
                    here = pl.ds(
                        pl.multiple_of((own_left if k == 0 else other_left) + i * 128, 128), 128
                    )
                    vrow[0:1, here] = vt[i : i + 1, :]
        full_h = h_buf[...]
        grads[0] = left[:, C : C + 1] * vrow[0:1, :] + dot(l_high, full_h) + dot(l_low, full_h)
        finish(h_a.values())
        finish(h_b)
        finish(h_c.values())


def shards(sn, sc, lv, emb, tim, gain, blk, rdo):
    vmem = pl.BlockSpec(memory_space=pltpu.VMEM)
    scratch = [
        ((C, ROWS), bf16), ((C, ROWS), bf16), ((ROWS // 128, 128), f32), ((1, C, D), bf16),
        ((1, D), f32), ((1, D), f32), ((1, DEPTH, F), bf16), ((1, C, F), bf16),
        ((80, F), f32), ((16, 128), f32), ((8, F), f32),
        ((SIDE, 16, HALF + 128), bf16), ((SIDE, 16, HALF + 128), bf16),
        ((16, HALF + 128), bf16), ((SIDE, 16, HALF + 128), bf16),
        ((2, 128, F), bf16), ((4, 16, 128), bf16), ((8, F), f32), ((ROWS, 128), f32),
        ((C, F), bf16), ((8, ROWS), f32), ((8, ROWS), f32),
        ((SIDE, 16, HALF + 128), bf16), ((SIDE, 16, HALF + 128), bf16),
        ((16, HALF + 128), bf16), ((SIDE, 16, HALF + 128), bf16),
        ((SIDE, 16, HALF + 128), bf16), ((C, F), bf16),
        ((2, F, 128), bf16), ((3, 128, 128), bf16), ((ROWS, 128), f32), ((ROWS, 128), f32),
        ((2, ROWS, 128), bf16), ((80, ROWS), bf16), ((2, ROWS, CHUNK), f32), ((ROWS, 128), f32),
        ((ROWS, F), f32), ((ROWS, F), f32),
        ((DEPTH, 128), f32), ((ROWS, 128), f32),
        ((ROWS, 128), f32),
        ((ROWS // 2, 128), bf16), ((ROWS // 2, 128), bf16), ((ROWS // 2, 128), bf16),
        ((4, ROWS // 2, 128), bf16),
    ]
    dma = pltpu.SemaphoreType.DMA
    grads, generated = pl.pallas_call(
        kernel,
        out_shape=(
            jax.ShapeDtypeStruct((1, DEPTH, F), f32),
            jax.ShapeDtypeStruct((C, ROWS), bf16),
        ),
        in_specs=[pl.BlockSpec(memory_space=pltpu.HBM)] * 8,
        out_specs=(vmem, vmem),
        scratch_shapes=[pltpu.VMEM(shape, kind) for shape, kind in scratch]
        + [dma((8,))]
        + [dma((3, SIDE)) for _ in range(4)]
        + [dma((1,)), dma((1,)), dma((1,)), dma((4,)), dma((13,)), dma((13,))]
        + [pltpu.SemaphoreType.REGULAR],
        compiler_params=pltpu.CompilerParams(
            collective_id=0, has_side_effects=True, vmem_limit_bytes=32 * 2**20
        ),
    )(
        *(
            pltpu.with_memory_space_constraint(array, pltpu.HBM)
            for array in (
                sn.T, sc.T, lv.reshape(ROWS // 128, 128), emb, tim, gain, blk,
                rdo.transpose(0, 2, 1),
            )
        )
    )
    return grads, generated.T


def solution(mesh):
    in_specs = (
        P("fsdp", None),
        P("fsdp", None),
        P("fsdp"),
        P("role", None, None),
        P("role", None),
        P("role", None),
        P("role", "fsdp", None),
        P("role", None, None),
    )
    out_specs = (P("role", "fsdp", None), P("fsdp", None))
    return jax.shard_map(shards, mesh=mesh, in_specs=in_specs, out_specs=out_specs, check_vma=False)
```
